128 devices in a mesh: dp: 32 (over y, z, core), tensor: 4 (over x).
Axes of the slice: x: 4, y: 4, z: 4, core: 2. Of those that a mesh axis runs over, the one named last changes fastest.
Arguments:
- queries: bfloat16 [49152, 4096], P(('dp', 'tensor')), may hold values from -6 to 6
- key_matrix: bfloat16 [49152, 512], P(('dp', 'tensor')), may hold values from -6 to 6
- value_matrix: bfloat16 [49152, 512], P(('dp', 'tensor')), may hold values from -6 to 6
- out_grads: bfloat16 [49152, 4096], P(('dp', 'tensor')), may hold values from -6 to 6
- seg_ids: int32 [96, 512], P('dp'), may hold values from 0 to 2, as said below
- bucket_dest: int32 [32, 3], P('dp'), may hold values from -1 to 31, as said below
Outputs:
- query_gradient_rows: bfloat16 [49152, 4096], P(('dp', 'tensor'))
- key_gradient_rows: bfloat16 [49152, 512], P(('dp', 'tensor'))
- value_gradient_rows: bfloat16 [49152, 512], P(('dp', 'tensor'))
The draws below stay inside these ranges and needn't reach their ends.
Inputs may be any that keep to these rules, and one draw needn't show every extreme that they name: `seg_ids`: each pack holds three documents in row order with numbers 0, 1, 2, each of two rows or more; one of them has exactly 256 rows. `bucket_dest`: -1 marks an empty pack. Index r and its partner, the index half the axis away (r + 32 / 2 modulo 32), form a pair: in every pair one index has three live packs, one naming itself and two naming its partner, in any order, and the other index has one live pack, in any slot, which names its partner. So every index works on exactly two packs.
All inputs are finite; a program needn't handle non-finite values.
Results may differ from the reference program's by a relative error of at most 0.0049.
Values may be sent and summed in bfloat16 or wider, within the bound.
A program may use at most 128 MiB of HBM per device.

```python
import math
import jax
import jax.numpy as jnp
from jax import lax

LOCAL_QUERY_HEADS = 32
LOCAL_KEY_HEADS = 4
HEAD_SIZE = 128
PACK_ROWS = 512
PACKS_PER_RANK = 3
TOTAL_ROWS = 49152
N_DP = 32


def draw_queries(key, part):
    key = jax.random.fold_in(key, 1)
    value_entries = jnp.clip(jax.random.normal(key, (N_DP * PACKS_PER_RANK * PACK_ROWS, LOCAL_QUERY_HEADS * HEAD_SIZE)), -6.0, 6.0)
    return value_entries.astype(jnp.bfloat16)


def draw_key_matrix(key, part):
    key = jax.random.fold_in(key, 2)
    value_entries = jnp.clip(jax.random.normal(key, (N_DP * PACKS_PER_RANK * PACK_ROWS, LOCAL_KEY_HEADS * HEAD_SIZE)), -6.0, 6.0)
    return value_entries.astype(jnp.bfloat16)


def draw_seg_ids(key, part):
    key = jax.random.fold_in(key, 3)
    bucket_count = N_DP * PACKS_PER_RANK
    longest = PACK_ROWS // 2
    spare = PACK_ROWS - longest
    first_short = jax.random.randint(jax.random.fold_in(key, 1), (bucket_count,), 2, spare - 1)
    second_short = spare - first_short
    placed = jax.random.randint(jax.random.fold_in(key, 2), (bucket_count,), 0, 3)
    first_length = jnp.where(placed == 0, longest, first_short)
    length_two = jnp.where(placed == 1, longest, jnp.where(placed == 0, first_short, second_short))
    border_one = first_length
    border_two = first_length + length_two
    columns = jnp.arange(PACK_ROWS, dtype=jnp.int32)
    segments = (columns[None, :] >= border_one[:, None]).astype(jnp.int32) + (columns[None, :] >= border_two[:, None]).astype(jnp.int32)
    return segments.astype(jnp.int32)


def draw_bucket_dest(key, part):
    key = jax.random.fold_in(key, 5)
    half = N_DP // 2
    heavy_low = jax.random.randint(jax.random.fold_in(key, 1), (half,), 0, 2).astype(jnp.int32)
    heavy_low = heavy_low.at[0].set(1).at[1].set(0)
    self_slot = jax.random.randint(jax.random.fold_in(key, 2), (half,), 0, 3).astype(jnp.int32)
    light_slot = jax.random.randint(jax.random.fold_in(key, 4), (half,), 0, 3).astype(jnp.int32)
    slots = jnp.arange(3, dtype=jnp.int32)
    low_index = jnp.arange(half, dtype=jnp.int32)[:, None]
    high_index = low_index + half
    empty = -jnp.ones((half, 3), jnp.int32)
    self_here = slots[None, :] == self_slot[:, None]
    light_here = slots[None, :] == light_slot[:, None]
    heavy_for_low = jnp.where(self_here, low_index, high_index)
    heavy_for_high = jnp.where(self_here, high_index, low_index)
    light_for_low = jnp.where(light_here, high_index, empty)
    light_for_high = jnp.where(light_here, low_index, empty)
    flag = (heavy_low == 1)[:, None]
    low_rows = jnp.where(flag, heavy_for_low, light_for_low)
    upper_rows = jnp.where(flag, light_for_high, heavy_for_high)
    return jnp.concatenate([low_rows, upper_rows], axis=0).astype(jnp.int32)


def block_levels(key, dims, shards, least, high):
    level = 1.0
    for dim, shards_of in shards:
        draws = jax.random.uniform(jax.random.fold_in(jax.random.fold_in(key, 6), dim), (shards_of,), jnp.float32, least / len(shards), high / len(shards))
        level = level * jnp.repeat(jnp.exp(draws), dims[dim] // shards_of).reshape((-1,) + (1,) * (len(dims) - 1 - dim))
    return level


def normal_values(rng, shape, deviation, bound, split=(), held_as=jnp.bfloat16):
    result = deviation * jax.random.normal(rng, shape, jnp.float32)
    if split:
        result = result * block_levels(rng, shape, split, -0.22, 0.18)
    return jnp.clip(result, -bound, bound).astype(held_as)


def setup_inputs(seed: int = 0) -> dict:
    seeds = jax.random.split(jax.random.key(seed), 7)
    return {
        "queries": draw_queries(jax.random.fold_in(seeds[6], 71), 0),
        "key_matrix": draw_key_matrix(jax.random.fold_in(seeds[6], 71), 0),
        "value_matrix": normal_values(seeds[2], (TOTAL_ROWS, LOCAL_KEY_HEADS * HEAD_SIZE), 1.0, 6.0, ((0, 128),)),
        "out_grads": normal_values(seeds[3], (TOTAL_ROWS, LOCAL_QUERY_HEADS * HEAD_SIZE), 1.0, 6.0, ((0, 128),)),
        "seg_ids": draw_seg_ids(jax.random.fold_in(seeds[6], 71), 0),
        "bucket_dest": draw_bucket_dest(jax.random.fold_in(seeds[6], 71), 0),
    }


def bucket_grads(bucket_queries, bucket_keys, bucket_values, bucketed_output_rows, segments):
    count_of_rows = bucket_queries.shape[0]
    group_width = LOCAL_QUERY_HEADS // LOCAL_KEY_HEADS
    scale_factor = 1.0 / math.sqrt(HEAD_SIZE)
    query_float = bucket_queries.reshape(count_of_rows, LOCAL_KEY_HEADS, group_width, HEAD_SIZE).astype(jnp.float32)
    key_float = bucket_keys.reshape(count_of_rows, LOCAL_KEY_HEADS, HEAD_SIZE).astype(jnp.float32)
    value_float = bucket_values.reshape(count_of_rows, LOCAL_KEY_HEADS, HEAD_SIZE).astype(jnp.float32)
    gradient_function = bucketed_output_rows.reshape(count_of_rows, LOCAL_KEY_HEADS, group_width, HEAD_SIZE).astype(jnp.float32)
    scores = jnp.einsum('qhgd,khd->hgqk', query_float, key_float) * scale_factor
    position = jnp.arange(count_of_rows)
    allowed = (segments[:, None] == segments[None, :]) & (position[None, :] <= position[:, None])
    masked_scores = jnp.where(allowed, scores, -jnp.inf)
    row_max = lax.optimization_barrier(jnp.max(masked_scores, axis=-1, keepdims=True))
    weights = jnp.where(allowed, jnp.exp(scores - row_max), 0.0)
    probs = weights / lax.optimization_barrier(jnp.sum(weights, axis=-1, keepdims=True))
    probs_half = lax.optimization_barrier(probs.astype(jnp.bfloat16)).astype(jnp.float32)
    dprobs = jnp.einsum('qhgd,khd->hgqk', gradient_function, value_float)
    delta = lax.optimization_barrier(jnp.sum(probs * dprobs, axis=-1, keepdims=True))
    dscores = lax.optimization_barrier((probs * (dprobs - delta)).astype(jnp.bfloat16)).astype(jnp.float32)
    query_gradient = jnp.einsum('hgqk,khd->qhgd', dscores, key_float) * scale_factor
    key_gradient = jnp.einsum('hgqk,qhgd->khd', dscores, query_float) * scale_factor
    value_gradient = jnp.einsum('hgqk,qhgd->khd', probs_half, gradient_function)
    return (query_gradient.reshape(count_of_rows, LOCAL_QUERY_HEADS * HEAD_SIZE).astype(jnp.bfloat16), key_gradient.reshape(count_of_rows, LOCAL_KEY_HEADS * HEAD_SIZE).astype(jnp.bfloat16), value_gradient.reshape(count_of_rows, LOCAL_KEY_HEADS * HEAD_SIZE).astype(jnp.bfloat16))

def reference(queries, key_matrix, value_matrix, out_grads, seg_ids, bucket_dest):
    bucket_list = N_DP * PACKS_PER_RANK
    query_b = queries.reshape(bucket_list, PACK_ROWS, LOCAL_QUERY_HEADS * HEAD_SIZE)
    key_bucketed = key_matrix.reshape(bucket_list, PACK_ROWS, LOCAL_KEY_HEADS * HEAD_SIZE)
    value_bucketed = value_matrix.reshape(bucket_list, PACK_ROWS, LOCAL_KEY_HEADS * HEAD_SIZE)
    grad_b = out_grads.reshape(bucket_list, PACK_ROWS, LOCAL_QUERY_HEADS * HEAD_SIZE)

    def one_bucket(operands):
        return bucket_grads(*operands)
    query_all, key_all, value_all = lax.map(one_bucket, (query_b, key_bucketed, value_bucketed, grad_b, seg_ids))
    live = bucket_dest.reshape(bucket_list) >= 0
    zero = jnp.zeros((), jnp.bfloat16)
    query_gradient_rows = jnp.where(live[:, None, None], query_all, zero)
    key_gradient_rows = jnp.where(live[:, None, None], key_all, zero)
    value_gradient_rows = jnp.where(live[:, None, None], value_all, zero)
    return (query_gradient_rows.reshape(TOTAL_ROWS, LOCAL_QUERY_HEADS * HEAD_SIZE), key_gradient_rows.reshape(TOTAL_ROWS, LOCAL_KEY_HEADS * HEAD_SIZE), value_gradient_rows.reshape(TOTAL_ROWS, LOCAL_KEY_HEADS * HEAD_SIZE))
```

```python
import math

import jax
import jax.numpy as jnp
from jax import lax
from jax.experimental import pallas as pl
from jax.experimental.pallas import tpu as pltpu
from jax.sharding import PartitionSpec as P

HEAD = 128
GROUP = 8
KEYS = 4
BLOCK = 128
WINDOW = 3
MASKED = -1e30
MESH = pl.DeviceIdType.MESH
TASKS_FIRST, TASKS_LAST = 2, 2


def kernel(
    q_hbm, k_hbm, v_hbm, o_hbm, seg_ref, dest_ref,
    dq_ref, dk_ref, dv_ref,
    q_s, o_s, k_s, v_s, kt_s, bias_s, p_s, ds_s, dk_acc, dv_acc, k_out, v_out, k_in, v_in,
    load_sem, send_sem, recv_sem, back_send_sem, back_recv_sem,
):
    t = lax.axis_index("tensor")
    right, left = lax.rem(t + 1, 4), lax.rem(t + 3, 4)
    scale = 1.0 / math.sqrt(HEAD)
    exponent = scale * math.log2(math.e)

    def loads(c):
        wide = pl.ds(c * (GROUP * HEAD), GROUP * HEAD)
        narrow = pl.ds(c * HEAD, HEAD)
        return (
            pltpu.make_async_copy(k_hbm.at[:, narrow], k_s.at[c, pl.ds(256, 384)], load_sem.at[c, 0]),
            pltpu.make_async_copy(v_hbm.at[:, narrow], v_s.at[c, pl.ds(256, 384)], load_sem.at[c, 1]),
            pltpu.make_async_copy(q_hbm.at[:, wide], q_s.at[c], load_sem.at[c, 2]),
            pltpu.make_async_copy(o_hbm.at[:, wide], o_s.at[c], load_sem.at[c, 3]),
        )

    def remote(c):
        narrow = pl.ds(c * HEAD, HEAD)
        return (
            pltpu.make_async_remote_copy(
                k_hbm.at[pl.ds(128, 256), narrow], k_s.at[c, pl.ds(0, 256)],
                send_sem.at[c, 0], recv_sem.at[c, 0], device_id={"tensor": right}, device_id_type=MESH),
            pltpu.make_async_remote_copy(
                v_hbm.at[pl.ds(128, 256), narrow], v_s.at[c, pl.ds(0, 256)],
                send_sem.at[c, 1], recv_sem.at[c, 1], device_id={"tensor": right}, device_id_type=MESH),
        )

    def back(c):
        return (
            pltpu.make_async_remote_copy(
                k_out.at[c], k_in.at[c],
                back_send_sem.at[c, 0], back_recv_sem.at[c, 0], device_id={"tensor": left}, device_id_type=MESH),
            pltpu.make_async_remote_copy(
                v_out.at[c], v_in.at[c],
                back_send_sem.at[c, 1], back_recv_sem.at[c, 1], device_id={"tensor": left}, device_id_type=MESH),
        )

    for c in range(KEYS):
        for copy in loads(c):
            copy.start()
    barrier = pltpu.get_barrier_semaphore()
    for neighbour in (left, right):
        pl.semaphore_signal(barrier, inc=1, device_id={"tensor": neighbour}, device_id_type=MESH)

    for b in range(3):
        block = 3 * t + b
        pack = block // 4
        segs = seg_ref[pl.ds(pack, 1), :]
        first = jnp.sum((segs == 0).astype(jnp.int32), axis=1, keepdims=True)
        second = jnp.sum((segs <= 1).astype(jnp.int32), axis=1, keepdims=True)
        row = lax.broadcasted_iota(jnp.int32, (1, BLOCK), 1) + (block - 4 * pack) * BLOCK
        start = jnp.where(row >= second, second, jnp.where(row >= first, first, 0))
        key = lax.broadcasted_iota(jnp.int32, (WINDOW * BLOCK, BLOCK), 0) + (block - 4 * pack - 2) * BLOCK
        bias_s[b] = jnp.where((key >= start) & (key <= row), 0.0, MASKED)
    dk_acc[...] = jnp.zeros_like(dk_acc)
    dv_acc[...] = jnp.zeros_like(dv_acc)

    pl.semaphore_wait(barrier, 2)
    for c in range(KEYS):
        for copy in remote(c):
            copy.start()

    def live_scale(b):
        alive = dest_ref[0, (3 * t + b) // 4] >= 0
        return jnp.where(alive, 1.0, 0.0).astype(jnp.float32)

    def arrived(c):
        for copy in loads(c):
            copy.wait()
        for w in range(2, 5):
            kt_s[c, w] = k_s[c, pl.ds(w * BLOCK, BLOCK), :].T

    def step(b, c):
        rows = pl.ds(pl.multiple_of(b * BLOCK, BLOCK), BLOCK)
        window = pl.ds(pl.multiple_of(b * BLOCK, BLOCK), WINDOW * BLOCK)
        keys = k_s[c, window, :]
        values = v_s[c, window, :]
        bias = bias_s[b]
        bias = jnp.concatenate([bias, bias], axis=1)
        keys_t = jnp.concatenate([kt_s[c, b], kt_s[c, b + 1], kt_s[c, b + 2]], axis=1)
        factor = scale * live_scale(b)
        for pair in range(GROUP // 2):
            q2 = jnp.concatenate(
                [q_s[c, rows, (2 * pair + i) * HEAD : (2 * pair + i + 1) * HEAD] for i in range(2)], axis=0)
            o2 = jnp.concatenate(
                [o_s[c, rows, (2 * pair + i) * HEAD : (2 * pair + i + 1) * HEAD] for i in range(2)], axis=0)
            scores = lax.dot_general(keys, q2, (((1,), (1,)), ((), ())), preferred_element_type=jnp.float32)
            scores = scores + bias
            top = jnp.max(scores, axis=0, keepdims=True)
            weights = jnp.exp2((scores - top) * exponent)
            probs = weights * (1.0 / jnp.sum(weights, axis=0, keepdims=True))
            dprobs = lax.dot_general(values, o2, (((1,), (1,)), ((), ())), preferred_element_type=jnp.float32)
            delta = jnp.sum(probs * dprobs, axis=0, keepdims=True)
            dscores = (probs * (dprobs - delta)).astype(jnp.bfloat16)
            columns = slice(pair * 2 * HEAD, (pair + 1) * 2 * HEAD)
            p_s[:, columns] = probs.astype(jnp.bfloat16)
            ds_s[:, columns] = dscores
            dq_t = jnp.dot(keys_t, dscores, preferred_element_type=jnp.float32) * factor
            dq = dq_t.astype(jnp.bfloat16).T
            for i in range(2):
                at = pl.multiple_of(c * (GROUP * HEAD) + (2 * pair + i) * HEAD, HEAD)
                dq_ref[rows, pl.ds(at, HEAD)] = dq[i * BLOCK : (i + 1) * BLOCK]
        q8 = jnp.concatenate([q_s[c, rows, h * HEAD : (h + 1) * HEAD] for h in range(GROUP)], axis=0)
        o8 = jnp.concatenate([o_s[c, rows, h * HEAD : (h + 1) * HEAD] for h in range(GROUP)], axis=0)
        dk_acc[c, window, :] += jnp.dot(ds_s[...], q8, preferred_element_type=jnp.float32)
        dv_acc[c, window, :] += jnp.dot(p_s[...], o8, preferred_element_type=jnp.float32)

    def first_body(c, carry):
        arrived(c)
        step(2, c)
        return carry

    def middle_body(c, carry):
        @pl.when(c >= TASKS_FIRST)
        def _():
            arrived(c)

        for copy in remote(c):
            copy.wait_recv()
        for w in range(2):
            kt_s[c, w] = k_s[c, pl.ds(w * BLOCK, BLOCK), :].T

        def inner(b, carry):
            step(b, c)
            return carry

        lax.fori_loop(0, 2, inner, 0)
        k_out[c] = (dk_acc[c, pl.ds(0, 256), :] * scale).astype(jnp.bfloat16)
        v_out[c] = dv_acc[c, pl.ds(0, 256), :].astype(jnp.bfloat16)
        for copy in back(c):
            copy.start()
        return carry

    def last_body(c, carry):
        step(2, c)
        return carry

    lax.fori_loop(0, TASKS_FIRST, first_body, 0)
    lax.fori_loop(0, KEYS, middle_body, 0)
    lax.fori_loop(KEYS - TASKS_LAST, KEYS, last_body, 0)

    for c in range(KEYS):
        for copy in back(c):
            copy.wait()
        for b in range(3):
            rows = pl.ds((b + 2) * BLOCK, BLOCK)
            dk = dk_acc[c, rows, :] * scale
            dv = dv_acc[c, rows, :]
            if b:
                dk = dk + k_in[c, pl.ds((b - 1) * BLOCK, BLOCK), :].astype(jnp.float32)
                dv = dv + v_in[c, pl.ds((b - 1) * BLOCK, BLOCK), :].astype(jnp.float32)
            alive = live_scale(b)
            dk_ref[b * BLOCK : (b + 1) * BLOCK, c * HEAD : (c + 1) * HEAD] = (dk * alive).astype(jnp.bfloat16)
            dv_ref[b * BLOCK : (b + 1) * BLOCK, c * HEAD : (c + 1) * HEAD] = (dv * alive).astype(jnp.bfloat16)
    for c in range(KEYS):
        for copy in remote(c):
            copy.wait_send()


def local(queries, key_matrix, value_matrix, out_grads, seg_ids, bucket_dest):
    half, full = jnp.bfloat16, jnp.float32
    rows, q_width = queries.shape
    kv_width = key_matrix.shape[1]
    return pl.pallas_call(
        kernel,
        out_shape=(
            jax.ShapeDtypeStruct((rows, q_width), half),
            jax.ShapeDtypeStruct((rows, kv_width), half),
            jax.ShapeDtypeStruct((rows, kv_width), half),
        ),
        in_specs=[pl.BlockSpec(memory_space=pl.ANY)] * 4
        + [pl.BlockSpec(memory_space=pltpu.VMEM), pl.BlockSpec(memory_space=pltpu.SMEM)],
        out_specs=[pl.BlockSpec(memory_space=pltpu.VMEM)] * 3,
        scratch_shapes=[
            pltpu.VMEM((KEYS, rows, GROUP * HEAD), half),
            pltpu.VMEM((KEYS, rows, GROUP * HEAD), half),
            pltpu.VMEM((KEYS, rows + 256, HEAD), half),
            pltpu.VMEM((KEYS, rows + 256, HEAD), half),
            pltpu.VMEM((KEYS, 5, HEAD, BLOCK), half),
            pltpu.VMEM((3, WINDOW * BLOCK, BLOCK), full),
            pltpu.VMEM((WINDOW * BLOCK, GROUP * HEAD), half),
            pltpu.VMEM((WINDOW * BLOCK, GROUP * HEAD), half),
            pltpu.VMEM((KEYS, rows + 256, HEAD), full),
            pltpu.VMEM((KEYS, rows + 256, HEAD), full),
            pltpu.VMEM((KEYS, 256, HEAD), half),
            pltpu.VMEM((KEYS, 256, HEAD), half),
            pltpu.VMEM((KEYS, 256, HEAD), half),
            pltpu.VMEM((KEYS, 256, HEAD), half),
            pltpu.SemaphoreType.DMA((KEYS, 4)),
            pltpu.SemaphoreType.DMA((KEYS, 2)),
            pltpu.SemaphoreType.DMA((KEYS, 2)),
            pltpu.SemaphoreType.DMA((KEYS, 2)),
            pltpu.SemaphoreType.DMA((KEYS, 2)),
        ],
        compiler_params=pltpu.CompilerParams(
            collective_id=0, has_side_effects=True, vmem_limit_bytes=56 * 1024 * 1024
        ),
        name="packed_attention_backward",
    )(queries, key_matrix, value_matrix, out_grads, seg_ids, bucket_dest)


def solution(mesh):
    in_specs = (
        P(("dp", "tensor"), None),
        P(("dp", "tensor"), None),
        P(("dp", "tensor"), None),
        P(("dp", "tensor"), None),
        P("dp", None),
        P("dp", None),
    )
    out_specs = (P(("dp", "tensor"), None), P(("dp", "tensor"), None), P(("dp", "tensor"), None))
    return jax.shard_map(local, mesh=mesh, in_specs=in_specs, out_specs=out_specs, check_vma=False)
```

```python
import math

import jax
import jax.numpy as jnp
from jax import lax
from jax.experimental import pallas as pl
from jax.experimental.pallas import tpu as pltpu
from jax.sharding import PartitionSpec as P

HEAD = 128
GROUP = 8
KEYS = 4
BLOCK = 128
SUB = 32
WINDOW = 256 + SUB
MASKED = -1e30
MESH = pl.DeviceIdType.MESH


def kernel(
    q_hbm, k_hbm, v_hbm, o_hbm, seg_hbm, dest_hbm,
    dq_ref, dk_ref, dv_ref,
    q_s, o_s, k_s, v_s, kt_s, bias_s, s_buf, dp_buf, p_s, ds_s, dk_acc, dv_acc, k_out, v_out, k_in, v_in,
    seg_ref, dest_ref, load_sem, small_sem, send_sem, recv_sem, back_send_sem, back_recv_sem,
):
    t = lax.axis_index("tensor")
    right, left = lax.rem(t + 1, 4), lax.rem(t + 3, 4)
    scale = 1.0 / math.sqrt(HEAD)
    exponent = scale * math.log2(math.e)

    def loads(c):
        wide = pl.ds(c * (GROUP * HEAD), GROUP * HEAD)
        narrow = pl.ds(c * HEAD, HEAD)
        return (
            pltpu.make_async_copy(k_hbm.at[:, narrow], k_s.at[c, pl.ds(256, 384)], load_sem.at[c, 0]),
            pltpu.make_async_copy(v_hbm.at[:, narrow], v_s.at[c, pl.ds(256, 384)], load_sem.at[c, 1]),
            pltpu.make_async_copy(q_hbm.at[:, wide], q_s.at[c], load_sem.at[c, 2]),
            pltpu.make_async_copy(o_hbm.at[:, wide], o_s.at[c], load_sem.at[c, 3]),
        )

    def remote(c):
        narrow = pl.ds(c * HEAD, HEAD)
        return (
            pltpu.make_async_remote_copy(
                k_hbm.at[pl.ds(128, 256), narrow], k_s.at[c, pl.ds(0, 256)],
                send_sem.at[c, 0], recv_sem.at[c, 0], device_id={"tensor": right}, device_id_type=MESH),
            pltpu.make_async_remote_copy(
                v_hbm.at[pl.ds(128, 256), narrow], v_s.at[c, pl.ds(0, 256)],
                send_sem.at[c, 1], recv_sem.at[c, 1], device_id={"tensor": right}, device_id_type=MESH),
        )

    def back(c):
        return (
            pltpu.make_async_remote_copy(
                k_out.at[c], k_in.at[c],
                back_send_sem.at[c, 0], back_recv_sem.at[c, 0], device_id={"tensor": left}, device_id_type=MESH),
            pltpu.make_async_remote_copy(
                v_out.at[c], v_in.at[c],
                back_send_sem.at[c, 1], back_recv_sem.at[c, 1], device_id={"tensor": left}, device_id_type=MESH),
        )

    for c in range(KEYS):
        for copy in loads(c):
            copy.start()
    small = (
        pltpu.make_async_copy(seg_hbm, seg_ref, small_sem.at[0]),
        pltpu.make_async_copy(dest_hbm, dest_ref, small_sem.at[1]),
    )
    for copy in small:
        copy.start()
    barrier = pltpu.get_barrier_semaphore()
    for neighbour in (left, right):
        pl.semaphore_signal(barrier, inc=1, device_id={"tensor": neighbour}, device_id_type=MESH)

    for copy in small:
        copy.wait()
    for b in range(3):
        block = 3 * t + b
        pack = block // 4
        segs = seg_ref[pl.ds(pack, 1), :]
        first = jnp.sum((segs == 0).astype(jnp.int32), axis=1, keepdims=True)
        second = jnp.sum((segs <= 1).astype(jnp.int32), axis=1, keepdims=True)
        for sub in range(4):
            base = (block - 4 * pack) * BLOCK + sub * SUB
            row = lax.rem(lax.broadcasted_iota(jnp.int32, (1, 4 * SUB), 1), SUB) + base
            start = jnp.where(row >= second, second, jnp.where(row >= first, first, 0))
            key = lax.broadcasted_iota(jnp.int32, (WINDOW, 4 * SUB), 0) + (base - 256)
            bias_s[b * 4 + sub] = jnp.where((key >= start) & (key <= row), 0.0, MASKED)
    dk_acc[...] = jnp.zeros_like(dk_acc)
    dv_acc[...] = jnp.zeros_like(dv_acc)
    p_s[1] = jnp.zeros_like(p_s[1])
    ds_s[1] = jnp.zeros_like(ds_s[1])

    pl.semaphore_wait(barrier, 2)
    for c in range(KEYS):
        for copy in remote(c):
            copy.start()

    def live_scale(b):
        alive = dest_ref[0, (3 * t + b) // 4] >= 0
        return jnp.where(alive, 1.0, 0.0).astype(jnp.float32)

    def arrived(c):
        for copy in loads(c):
            copy.wait()
        keys_transposed(c, 2, 5)

    def rows_of(b, sub):
        return pl.ds(pl.multiple_of(b * BLOCK + sub * SUB, SUB), SUB)

    def window_of(b, sub):
        return pl.ds(pl.multiple_of(b * BLOCK + sub * SUB, SUB), WINDOW)

    def stacked(ref, b, sub, c):
        rows = rows_of(b, sub)
        return jnp.concatenate([ref[c, rows, h * HEAD : (h + 1) * HEAD] for h in range(GROUP)], axis=0)

    def scores_of(b, sub, c):
        window = window_of(b, sub)
        s_buf[sub % 2] = lax.dot_general(
            k_s[c, window, :], stacked(q_s, b, sub, c), (((1,), (1,)), ((), ())), preferred_element_type=jnp.float32)
        dp_buf[sub % 2] = lax.dot_general(
            v_s[c, window, :], stacked(o_s, b, sub, c), (((1,), (1,)), ((), ())), preferred_element_type=jnp.float32)

    def softmax_of(b, sub):
        slot = sub % 2
        bias = bias_s[b * 4 + sub]
        for i in range(2):
            lanes = slice(i * HEAD, (i + 1) * HEAD)
            scores = s_buf[slot, :, lanes] + bias
            top = jnp.max(scores, axis=0, keepdims=True)
            weights = jnp.exp2((scores - top) * exponent)
            probs = weights * (1.0 / jnp.sum(weights, axis=0, keepdims=True))
            p_s[slot, :, lanes] = probs.astype(jnp.bfloat16)
            delta = jnp.sum(probs * dp_buf[slot, :, lanes], axis=0, keepdims=True)
            ds_s[slot, :, lanes] = (probs * (dp_buf[slot, :, lanes] - delta)).astype(jnp.bfloat16)

    def gradients(b, sub, c):
        slot = sub % 2
        rows, window = rows_of(b, sub), window_of(b, sub)
        dq_t = jnp.dot(
            jnp.concatenate([kt_s[c, sub, b], kt_s[c, sub, b + 1]], axis=1), ds_s[slot, : 2 * BLOCK, :],
            preferred_element_type=jnp.float32)
        dq_t = dq_t + jnp.dot(
            kt_s[c, sub, b + 2, :, :SUB], ds_s[slot, 2 * BLOCK :, :], preferred_element_type=jnp.float32)
        dq = (dq_t * (scale * live_scale(b))).astype(jnp.bfloat16).T
        for h in range(GROUP):
            at = pl.multiple_of(c * (GROUP * HEAD) + h * HEAD, HEAD)
            dq_ref[rows, pl.ds(at, HEAD)] = dq[h * SUB : (h + 1) * SUB]
        dk_acc[c, window, :] += jnp.dot(
            ds_s[slot], stacked(q_s, b, sub, c), preferred_element_type=jnp.float32)
        dv_acc[c, window, :] += jnp.dot(
            p_s[slot], stacked(o_s, b, sub, c), preferred_element_type=jnp.float32)

    def task(b, c, b_old, c_old):
        scores_of(b, 0, c)
        for sub in range(4):
            if sub < 3:
                scores_of(b, sub + 1, c)
            if sub:
                gradients(b, sub - 1, c)
            else:
                gradients(b_old, 3, c_old)
            softmax_of(b, sub)

    def keys_transposed(c, first, last):
        for sub in range(4):
            for w in range(first, last):
                at = w * BLOCK + sub * SUB
                if at + BLOCK <= 640:
                    kt_s[c, sub, w] = k_s[c, pl.ds(at, BLOCK), :].T
                else:
                    kt_s[c, sub, w] = jnp.concatenate(
                        [k_s[c, pl.ds(at, 640 - at), :].T, jnp.zeros((HEAD, BLOCK - 640 + at), jnp.bfloat16)], axis=1)

    def remote_arrived(c):
        for copy in remote(c):
            copy.wait_recv()
        keys_transposed(c, 0, 2)

    def body(m, carry):
        middle = (m >= 1) & (m <= KEYS)
        b0 = jnp.where(middle, 0, 2)
        b1 = jnp.where(middle, 1, 2)
        c0 = jnp.where(middle, m - 1, jnp.where(m == 0, 0, 2))
        c1 = jnp.where(middle, m - 1, jnp.where(m == 0, 1, 3))
        b_old = jnp.where(m >= 2, 1, 2)
        c_old = jnp.where(m >= 2, m - 2, jnp.where(m == 1, 1, 0))

        @pl.when(m == 0)
        def _():
            arrived(0)
            arrived(1)

        @pl.when((m == 3) | (m == 4))
        def _():
            arrived(m - 1)

        @pl.when(middle)
        def _():
            remote_arrived(m - 1)

        task(b0, c0, b_old, c_old)

        @pl.when(m >= 2)
        def _():
            k_out[m - 2] = (dk_acc[m - 2, pl.ds(0, 256), :] * scale).astype(jnp.bfloat16)
            v_out[m - 2] = dv_acc[m - 2, pl.ds(0, 256), :].astype(jnp.bfloat16)
            for copy in back(m - 2):
                copy.start()

        task(b1, c1, b0, c0)
        return carry

    lax.fori_loop(0, KEYS + 2, body, 0)
    gradients(2, 3, 3)

    for c in range(KEYS):
        for copy in back(c):
            copy.wait()
        for b in range(3):
            rows = pl.ds((b + 2) * BLOCK, BLOCK)
            dk = dk_acc[c, rows, :] * scale
            dv = dv_acc[c, rows, :]
            if b:
                dk = dk + k_in[c, pl.ds((b - 1) * BLOCK, BLOCK), :].astype(jnp.float32)
                dv = dv + v_in[c, pl.ds((b - 1) * BLOCK, BLOCK), :].astype(jnp.float32)
            alive = live_scale(b)
            dk_ref[b * BLOCK : (b + 1) * BLOCK, c * HEAD : (c + 1) * HEAD] = (dk * alive).astype(jnp.bfloat16)
            dv_ref[b * BLOCK : (b + 1) * BLOCK, c * HEAD : (c + 1) * HEAD] = (dv * alive).astype(jnp.bfloat16)
    for c in range(KEYS):
        for copy in remote(c):
            copy.wait_send()


def write_out(q_in, k_in, v_in, q_out, k_out, v_out, sem):
    copies = []
    for i in range(4):
        rows = pl.ds(96 * i, 96)
        copies.append(pltpu.make_async_copy(q_in.at[rows], q_out.at[rows], sem.at[i]))
    copies.append(pltpu.make_async_copy(k_in, k_out, sem.at[4]))
    copies.append(pltpu.make_async_copy(v_in, v_out, sem.at[5]))
    for copy in copies:
        copy.start()
    for copy in copies:
        copy.wait()


def local(queries, key_matrix, value_matrix, out_grads, seg_ids, bucket_dest):
    half, full = jnp.bfloat16, jnp.float32
    rows, q_width = queries.shape
    kv_width = key_matrix.shape[1]
    parts = pl.pallas_call(
        kernel,
        out_shape=(
            pltpu.VMEM((rows, q_width), half),
            pltpu.VMEM((rows, kv_width), half),
            pltpu.VMEM((rows, kv_width), half),
        ),
        in_specs=[pl.BlockSpec(memory_space=pltpu.HBM)] * 6,
        out_specs=[pl.BlockSpec(memory_space=pltpu.VMEM)] * 3,
        scratch_shapes=[
            pltpu.VMEM((KEYS, rows, GROUP * HEAD), half),
            pltpu.VMEM((KEYS, rows, GROUP * HEAD), half),
            pltpu.VMEM((KEYS, rows + 256, HEAD), half),
            pltpu.VMEM((KEYS, rows + 256, HEAD), half),
            pltpu.VMEM((KEYS, 4, 5, HEAD, BLOCK), half),
            pltpu.VMEM((12, WINDOW, 4 * SUB), full),
            pltpu.VMEM((2, WINDOW, GROUP * SUB), full),
            pltpu.VMEM((2, WINDOW, GROUP * SUB), full),
            pltpu.VMEM((2, WINDOW, GROUP * SUB), half),
            pltpu.VMEM((2, WINDOW, GROUP * SUB), half),
            pltpu.VMEM((KEYS, rows + 256, HEAD), full),
            pltpu.VMEM((KEYS, rows + 256, HEAD), full),
            pltpu.VMEM((KEYS, 256, HEAD), half),
            pltpu.VMEM((KEYS, 256, HEAD), half),
            pltpu.VMEM((KEYS, 256, HEAD), half),
            pltpu.VMEM((KEYS, 256, HEAD), half),
            pltpu.VMEM((3, 512), jnp.int32),
            pltpu.SMEM((1, 3), jnp.int32),
            pltpu.SemaphoreType.DMA((KEYS, 4)),
            pltpu.SemaphoreType.DMA((2,)),
            pltpu.SemaphoreType.DMA((KEYS, 2)),
            pltpu.SemaphoreType.DMA((KEYS, 2)),
            pltpu.SemaphoreType.DMA((KEYS, 2)),
            pltpu.SemaphoreType.DMA((KEYS, 2)),
        ],
        compiler_params=pltpu.CompilerParams(
            collective_id=0, has_side_effects=True, vmem_limit_bytes=32 * 1024 * 1024
        ),
        name="packed_attention_backward",
    )(
        *[
            pltpu.with_memory_space_constraint(x, pltpu.HBM)
            for x in (queries, key_matrix, value_matrix, out_grads, seg_ids, bucket_dest)
        ]
    )
    return pl.pallas_call(
        write_out,
        out_shape=(
            jax.ShapeDtypeStruct((rows, q_width), half),
            jax.ShapeDtypeStruct((rows, kv_width), half),
            jax.ShapeDtypeStruct((rows, kv_width), half),
        ),
        in_specs=[pl.BlockSpec(memory_space=pltpu.VMEM)] * 3,
        out_specs=[pl.BlockSpec(memory_space=pltpu.HBM)] * 3,
        scratch_shapes=[pltpu.SemaphoreType.DMA((6,))],
        compiler_params=pltpu.CompilerParams(vmem_limit_bytes=4 * 1024 * 1024),
        name="write_out",
    )(*[pltpu.with_memory_space_constraint(p, pltpu.VMEM) for p in parts])


def solution(mesh):
    in_specs = (
        P(("dp", "tensor"), None),
        P(("dp", "tensor"), None),
        P(("dp", "tensor"), None),
        P(("dp", "tensor"), None),
        P("dp", None),
        P("dp", None),
    )
    out_specs = (P(("dp", "tensor"), None), P(("dp", "tensor"), None), P(("dp", "tensor"), None))
    return jax.shard_map(local, mesh=mesh, in_specs=in_specs, out_specs=out_specs, check_vma=False)
```

```python
import math

import jax
import jax.numpy as jnp
from jax import lax
from jax.experimental import pallas as pl
from jax.experimental.pallas import tpu as pltpu
from jax.sharding import PartitionSpec as P

HEAD = 128
GROUP = 8
KEYS = 4
BLOCK = 128
SUB = 32
WINDOW = 256 + SUB
MASKED = -1e30
MESH = pl.DeviceIdType.MESH


def kernel(
    q_hbm, k_hbm, v_hbm, o_hbm, seg_hbm, dest_hbm,
    dq_ref, dk_ref, dv_ref,
    q_s, o_s, k_s, v_s, kt_s, bias_s, s_buf, dp_buf, p_s, ds_s, dk_acc, dv_acc, k_out, v_out, k_in, v_in,
    seg_ref, dest_ref, load_sem, small_sem, send_sem, recv_sem, back_send_sem, back_recv_sem,
):
    t = lax.axis_index("tensor")
    right, left = lax.rem(t + 1, 4), lax.rem(t + 3, 4)
    scale = 1.0 / math.sqrt(HEAD)
    exponent = scale * math.log2(math.e)

    def loads(c):
        wide = pl.ds(c * (GROUP * HEAD), GROUP * HEAD)
        narrow = pl.ds(c * HEAD, HEAD)
        return (
            pltpu.make_async_copy(k_hbm.at[:, narrow], k_s.at[c, pl.ds(256, 384)], load_sem.at[c, 0]),
            pltpu.make_async_copy(v_hbm.at[:, narrow], v_s.at[c, pl.ds(256, 384)], load_sem.at[c, 1]),
            pltpu.make_async_copy(q_hbm.at[:, wide], q_s.at[c], load_sem.at[c, 2]),
            pltpu.make_async_copy(o_hbm.at[:, wide], o_s.at[c], load_sem.at[c, 3]),
        )

    sends = (t < 2, t < 3)
    receives = ((t == 1) | (t == 2), t > 0)

    def remote(c, part):
        narrow = pl.ds(c * HEAD, HEAD)
        there, here = pl.ds((part + 1) * BLOCK, BLOCK), pl.ds(part * BLOCK, BLOCK)
        return (
            pltpu.make_async_remote_copy(
                k_hbm.at[there, narrow], k_s.at[c, here], send_sem.at[c, part, 0], recv_sem.at[c, part, 0],
                device_id={"tensor": right}, device_id_type=MESH),
            pltpu.make_async_remote_copy(
                v_hbm.at[there, narrow], v_s.at[c, here], send_sem.at[c, part, 1], recv_sem.at[c, part, 1],
                device_id={"tensor": right}, device_id_type=MESH),
        )

    def back(c, part):
        rows = pl.ds(part * BLOCK, BLOCK)
        return (
            pltpu.make_async_remote_copy(
                k_out.at[c, rows], k_in.at[c, rows], back_send_sem.at[c, part, 0], back_recv_sem.at[c, part, 0],
                device_id={"tensor": left}, device_id_type=MESH),
            pltpu.make_async_remote_copy(
                v_out.at[c, rows], v_in.at[c, rows], back_send_sem.at[c, part, 1], back_recv_sem.at[c, part, 1],
                device_id={"tensor": left}, device_id_type=MESH),
        )

    def send_back(c, part):
        rows = pl.ds(part * BLOCK, BLOCK)
        k_out[c, rows, :] = (dk_acc[c, rows, :] * scale).astype(jnp.bfloat16)
        v_out[c, rows, :] = dv_acc[c, rows, :].astype(jnp.bfloat16)
        for copy in back(c, part):
            copy.start()

    def send_first(c):
        @pl.when(receives[0])
        def _():
            send_back(c, 0)

        @pl.when(t == 1)
        def _():
            send_back(c, 1)

    def send_second(c):
        @pl.when(t >= 2)
        def _():
            send_back(c, 1)

    barrier = pltpu.get_barrier_semaphore()
    @pl.when(t > 0)
    def _():
        pl.semaphore_signal(barrier, inc=1, device_id={"tensor": left}, device_id_type=MESH)

    @pl.when(t < 3)
    def _():
        pl.semaphore_signal(barrier, inc=1, device_id={"tensor": right}, device_id_type=MESH)

    small = (
        pltpu.make_async_copy(seg_hbm, seg_ref, small_sem.at[0]),
        pltpu.make_async_copy(dest_hbm, dest_ref, small_sem.at[1]),
    )
    for copy in small:
        copy.start()
    for c in range(KEYS):
        for copy in loads(c):
            copy.start()
    @pl.when((t == 0) | (t == 3))
    def _():
        pl.semaphore_wait(barrier, 1)

    @pl.when((t == 1) | (t == 2))
    def _():
        pl.semaphore_wait(barrier, 2)

    for c in range(KEYS):
        for part in range(2):
            @pl.when(sends[part])
            def _():
                for copy in remote(c, part):
                    copy.start()

    for part in range(2):
        rows = slice(part * BLOCK, (part + 1) * BLOCK)

        @pl.when(jnp.logical_not(receives[part]))
        def _():
            k_s[:, rows, :] = jnp.zeros((KEYS, BLOCK, HEAD), jnp.bfloat16)
            v_s[:, rows, :] = jnp.zeros((KEYS, BLOCK, HEAD), jnp.bfloat16)

        @pl.when(jnp.logical_not(sends[part]))
        def _():
            k_in[:, rows, :] = jnp.zeros((KEYS, BLOCK, HEAD), jnp.bfloat16)
            v_in[:, rows, :] = jnp.zeros((KEYS, BLOCK, HEAD), jnp.bfloat16)

    for copy in small:
        copy.wait()
    for b in range(3):
        block = 3 * t + b
        pack = block // 4
        segs = seg_ref[pl.ds(pack, 1), :]
        first = jnp.sum((segs == 0).astype(jnp.int32), axis=1, keepdims=True)
        second = jnp.sum((segs <= 1).astype(jnp.int32), axis=1, keepdims=True)
        for sub in range(4):
            base = (block - 4 * pack) * BLOCK + sub * SUB
            row = lax.rem(lax.broadcasted_iota(jnp.int32, (1, 4 * SUB), 1), SUB) + base
            start = jnp.where(row >= second, second, jnp.where(row >= first, first, 0))
            key = lax.broadcasted_iota(jnp.int32, (WINDOW, 4 * SUB), 0) + (base - 256)
            bias_s[b * 4 + sub] = jnp.where((key >= start) & (key <= row), 0.0, MASKED)
    dk_acc[...] = jnp.zeros_like(dk_acc)
    dv_acc[...] = jnp.zeros_like(dv_acc)

    def live_scale(b):
        alive = dest_ref[0, (3 * t + b) // 4] >= 0
        return jnp.where(alive, 1.0, 0.0).astype(jnp.float32)

    def arrived(c):
        for copy in loads(c):
            copy.wait()
        keys_transposed(c, 2, 5)

    def rows_of(b, sub):
        return pl.ds(pl.multiple_of(b * BLOCK + sub * SUB, SUB), SUB)

    def window_of(b, sub):
        return pl.ds(pl.multiple_of(b * BLOCK + sub * SUB, SUB), WINDOW)

    def stacked(ref, b, sub, c):
        rows = rows_of(b, sub)
        return jnp.concatenate([ref[c, rows, h * HEAD : (h + 1) * HEAD] for h in range(GROUP)], axis=0)

    def scores_of(b, sub, c):
        window = window_of(b, sub)
        s_buf[sub % 2] = lax.dot_general(
            k_s[c, window, :], stacked(q_s, b, sub, c), (((1,), (1,)), ((), ())), preferred_element_type=jnp.float32)
        dp_buf[sub % 2] = lax.dot_general(
            v_s[c, window, :], stacked(o_s, b, sub, c), (((1,), (1,)), ((), ())), preferred_element_type=jnp.float32)

    def softmax_of(b, sub):
        slot = sub % 2
        bias = bias_s[b * 4 + sub]
        for i in range(2):
            lanes = slice(i * HEAD, (i + 1) * HEAD)
            scores = s_buf[slot, :, lanes] + bias
            top = jnp.max(scores, axis=0, keepdims=True)
            weights = jnp.exp2((scores - top) * exponent)
            probs = weights * (1.0 / jnp.sum(weights, axis=0, keepdims=True))
            p_s[slot, :, lanes] = probs.astype(jnp.bfloat16)
            delta = jnp.sum(probs * dp_buf[slot, :, lanes], axis=0, keepdims=True)
            ds_s[slot, :, lanes] = (probs * (dp_buf[slot, :, lanes] - delta)).astype(jnp.bfloat16)

    def gradients(b, sub, c):
        slot = sub % 2
        rows, window = rows_of(b, sub), window_of(b, sub)
        dq_t = jnp.dot(
            jnp.concatenate([kt_s[c, sub, b], kt_s[c, sub, b + 1]], axis=1), ds_s[slot, : 2 * BLOCK, :],
            preferred_element_type=jnp.float32)
        dq_t = dq_t + jnp.dot(
            kt_s[c, sub, b + 2, :, :SUB], ds_s[slot, 2 * BLOCK :, :], preferred_element_type=jnp.float32)
        dq = (dq_t * (scale * live_scale(b))).astype(jnp.bfloat16).T
        for h in range(GROUP):
            at = pl.multiple_of(c * (GROUP * HEAD) + h * HEAD, HEAD)
            dq_ref[rows, pl.ds(at, HEAD)] = dq[h * SUB : (h + 1) * SUB]
        dk_acc[c, window, :] += jnp.dot(
            ds_s[slot], stacked(q_s, b, sub, c), preferred_element_type=jnp.float32)
        dv_acc[c, window, :] += jnp.dot(
            p_s[slot], stacked(o_s, b, sub, c), preferred_element_type=jnp.float32)

    def task(b, c, old, between=None):
        for sub in range(4):
            if sub == 2 and between is not None:
                between()
            scores_of(b, sub, c)
            if sub >= 2:
                gradients(b, sub - 2, c)
            elif old is not None:
                gradients(old[0], sub + 2, old[1])
            if sub >= 1:
                softmax_of(b, sub - 1)
            elif old is not None:
                softmax_of(old[0], 3)

    def drain(b, c):
        gradients(b, 2, c)
        softmax_of(b, 3)
        gradients(b, 3, c)

    def keys_transposed(c, first, last):
        for sub in range(4):
            for w in range(first, last):
                at = w * BLOCK + sub * SUB
                if at + BLOCK <= 640:
                    kt_s[c, sub, w] = k_s[c, pl.ds(at, BLOCK), :].T
                else:
                    kt_s[c, sub, w] = jnp.concatenate(
                        [k_s[c, pl.ds(at, 640 - at), :].T, jnp.zeros((HEAD, BLOCK - 640 + at), jnp.bfloat16)], axis=1)

    def remote_arrived(c):
        for part in range(2):
            @pl.when(receives[part])
            def _():
                for copy in remote(c, part):
                    copy.wait_recv()

        keys_transposed(c, 0, 2)

    def place(n):
        early = n < 2
        return jnp.where(early, 2, lax.rem(n, 2)), jnp.where(early, n, lax.div(n - 2, 2))

    def body(n, carry):
        b, c = place(n)

        @pl.when(n < KEYS)
        def _():
            arrived(n)

        @pl.when((n >= 2) & (b == 0))
        def _():
            remote_arrived(c)

        task(b, c, place(n - 1))

        @pl.when((n >= 2) & (b == 1))
        def _():
            send_first(c)

        @pl.when((n >= 3) & (b == 0))
        def _():
            send_second(c - 1)

        return carry

    last = KEYS - 1
    arrived(0)
    task(2, 0, None)
    lax.fori_loop(1, 2 * KEYS + 1, body, 0)
    drain(0, last)
    send_first(last)
    task(1, last, None)
    drain(1, last)
    send_second(last)
    task(2, last - 1, None)
    task(2, last, (2, last - 1))
    drain(2, last)

    def result(c, b):
        rows = pl.ds((b + 2) * BLOCK, BLOCK)
        dk = dk_acc[c, rows, :] * scale
        dv = dv_acc[c, rows, :]
        if b:
            dk = dk + k_in[c, pl.ds((b - 1) * BLOCK, BLOCK), :].astype(jnp.float32)
            dv = dv + v_in[c, pl.ds((b - 1) * BLOCK, BLOCK), :].astype(jnp.float32)
        alive = live_scale(b)
        dk_ref[b * BLOCK : (b + 1) * BLOCK, c * HEAD : (c + 1) * HEAD] = (dk * alive).astype(jnp.bfloat16)
        dv_ref[b * BLOCK : (b + 1) * BLOCK, c * HEAD : (c + 1) * HEAD] = (dv * alive).astype(jnp.bfloat16)

    for c in range(KEYS):
        result(c, 0)
    for c in range(KEYS):
        for part in range(2):
            @pl.when(sends[part])
            def _():
                for copy in back(c, part):
                    copy.wait_recv()

            result(c, part + 1)

    for c in range(KEYS):
        for part in range(2):
            @pl.when(receives[part])
            def _():
                for copy in back(c, part):
                    copy.wait_send()

            @pl.when(sends[part])
            def _():
                for copy in remote(c, part):
                    copy.wait_send()


def write_out(q_in, k_in, v_in, q_out, k_out, v_out, sem):
    copies = []
    for i in range(4):
        rows = pl.ds(96 * i, 96)
        copies.append(pltpu.make_async_copy(q_in.at[rows], q_out.at[rows], sem.at[i]))
    copies.append(pltpu.make_async_copy(k_in, k_out, sem.at[4]))
    copies.append(pltpu.make_async_copy(v_in, v_out, sem.at[5]))
    for copy in copies:
        copy.start()
    for copy in copies:
        copy.wait()


def local(queries, key_matrix, value_matrix, out_grads, seg_ids, bucket_dest):
    half, full = jnp.bfloat16, jnp.float32
    rows, q_width = queries.shape
    kv_width = key_matrix.shape[1]
    parts = pl.pallas_call(
        kernel,
        out_shape=(
            pltpu.VMEM((rows, q_width), half),
            pltpu.VMEM((rows, kv_width), half),
            pltpu.VMEM((rows, kv_width), half),
        ),
        in_specs=[pl.BlockSpec(memory_space=pltpu.HBM)] * 6,
        out_specs=[pl.BlockSpec(memory_space=pltpu.VMEM)] * 3,
        scratch_shapes=[
            pltpu.VMEM((KEYS, rows, GROUP * HEAD), half),
            pltpu.VMEM((KEYS, rows, GROUP * HEAD), half),
            pltpu.VMEM((KEYS, rows + 256, HEAD), half),
            pltpu.VMEM((KEYS, rows + 256, HEAD), half),
            pltpu.VMEM((KEYS, 4, 5, HEAD, BLOCK), half),
            pltpu.VMEM((12, WINDOW, 4 * SUB), full),
            pltpu.VMEM((2, WINDOW, GROUP * SUB), full),
            pltpu.VMEM((2, WINDOW, GROUP * SUB), full),
            pltpu.VMEM((2, WINDOW, GROUP * SUB), half),
            pltpu.VMEM((2, WINDOW, GROUP * SUB), half),
            pltpu.VMEM((KEYS, rows + 256, HEAD), full),
            pltpu.VMEM((KEYS, rows + 256, HEAD), full),
            pltpu.VMEM((KEYS, 256, HEAD), half),
            pltpu.VMEM((KEYS, 256, HEAD), half),
            pltpu.VMEM((KEYS, 256, HEAD), half),
            pltpu.VMEM((KEYS, 256, HEAD), half),
            pltpu.VMEM((3, 512), jnp.int32),
            pltpu.SMEM((1, 3), jnp.int32),
            pltpu.SemaphoreType.DMA((KEYS, 4)),
            pltpu.SemaphoreType.DMA((2,)),
            pltpu.SemaphoreType.DMA((KEYS, 2, 2)),
            pltpu.SemaphoreType.DMA((KEYS, 2, 2)),
            pltpu.SemaphoreType.DMA((KEYS, 2, 2)),
            pltpu.SemaphoreType.DMA((KEYS, 2, 2)),
        ],
        compiler_params=pltpu.CompilerParams(
            collective_id=0, has_side_effects=True, vmem_limit_bytes=32 * 1024 * 1024
        ),
        name="packed_attention_backward",
    )(
        *[
            pltpu.with_memory_space_constraint(x, pltpu.HBM)
            for x in (queries, key_matrix, value_matrix, out_grads, seg_ids, bucket_dest)
        ]
    )
    return pl.pallas_call(
        write_out,
        out_shape=(
            jax.ShapeDtypeStruct((rows, q_width), half),
            jax.ShapeDtypeStruct((rows, kv_width), half),
            jax.ShapeDtypeStruct((rows, kv_width), half),
        ),
        in_specs=[pl.BlockSpec(memory_space=pltpu.VMEM)] * 3,
        out_specs=[pl.BlockSpec(memory_space=pltpu.HBM)] * 3,
        scratch_shapes=[pltpu.SemaphoreType.DMA((6,))],
        compiler_params=pltpu.CompilerParams(vmem_limit_bytes=4 * 1024 * 1024),
        name="write_out",
    )(*[pltpu.with_memory_space_constraint(p, pltpu.VMEM) for p in parts])


def solution(mesh):
    in_specs = (
        P(("dp", "tensor"), None),
        P(("dp", "tensor"), None),
        P(("dp", "tensor"), None),
        P(("dp", "tensor"), None),
        P("dp", None),
        P("dp", None),
    )
    out_specs = (P(("dp", "tensor"), None), P(("dp", "tensor"), None), P(("dp", "tensor"), None))
    return jax.shard_map(local, mesh=mesh, in_specs=in_specs, out_specs=out_specs, check_vma=False)
```

```python
import math

import jax
import jax.numpy as jnp
from jax import lax
from jax.experimental import pallas as pl
from jax.experimental.pallas import tpu as pltpu
from jax.sharding import PartitionSpec as P

HEAD = 128
GROUP = 8
KEYS = 4
BLOCK = 128
FIRST, SECOND, LATER = 0, 1, 2
SUB = 32
WINDOW = 256 + SUB
MASKED = -1e30
MESH = pl.DeviceIdType.MESH


def kernel(
    q_hbm, k_hbm, v_hbm, o_hbm, seg_hbm, dest_hbm,
    dq_ref, dk_ref, dv_ref,
    q_s, o_s, k_s, v_s, kt_s, bias_s, s_buf, dp_buf, p_s, ds_s, p_full, p_half, dk_acc, dv_acc, k_out, v_out, k_in, v_in,
    seg_ref, dest_ref, load_sem, small_sem, send_sem, recv_sem, back_send_sem, back_recv_sem,
):
    t = lax.axis_index("tensor")
    right, left = lax.rem(t + 1, 4), lax.rem(t + 3, 4)
    scale = 1.0 / math.sqrt(HEAD)
    exponent = scale * math.log2(math.e)

    def loads(c):
        wide = pl.ds(c * (GROUP * HEAD), GROUP * HEAD)
        narrow = pl.ds(c * HEAD, HEAD)
        return (
            pltpu.make_async_copy(k_hbm.at[:, narrow], k_s.at[c, pl.ds(256, 384)], load_sem.at[c, 0]),
            pltpu.make_async_copy(v_hbm.at[:, narrow], v_s.at[c, pl.ds(256, 384)], load_sem.at[c, 1]),
            pltpu.make_async_copy(q_hbm.at[:, wide], q_s.at[c], load_sem.at[c, 2]),
            pltpu.make_async_copy(o_hbm.at[:, wide], o_s.at[c], load_sem.at[c, 3]),
        )

    sends = (t < 2, t < 3)
    receives = ((t == 1) | (t == 2), t > 0)

    def remote(c, part, which=(0, 1)):
        narrow = pl.ds(c * HEAD, HEAD)
        there, here = pl.ds((part + 1) * BLOCK, BLOCK), pl.ds(part * BLOCK, BLOCK)
        return [
            pltpu.make_async_remote_copy(
                source.at[there, narrow], target.at[c, here], send_sem.at[c, part, i], recv_sem.at[c, part, i],
                device_id={"tensor": right}, device_id_type=MESH)
            for i, (source, target) in enumerate(((k_hbm, k_s), (v_hbm, v_s))) if i in which
        ]

    def back(c, part, which=(0, 1)):
        rows = pl.ds(part * BLOCK, BLOCK)
        return [
            pltpu.make_async_remote_copy(
                source.at[c, rows], target.at[c, rows], back_send_sem.at[c, part, i], back_recv_sem.at[c, part, i],
                device_id={"tensor": left}, device_id_type=MESH)
            for i, (source, target) in enumerate(((k_out, k_in), (v_out, v_in))) if i in which
        ]

    def send_back(c, part, which):
        rows = pl.ds(part * BLOCK, BLOCK)
        if 0 in which:
            k_out[c, rows, :] = (dk_acc[c, rows, :] * scale).astype(jnp.bfloat16)
        if 1 in which:
            v_out[c, rows, :] = dv_acc[c, rows, :].astype(jnp.bfloat16)
        for copy in back(c, part, which):
            copy.start()

    barrier = pltpu.get_barrier_semaphore()
    @pl.when(t > 0)
    def _():
        pl.semaphore_signal(barrier, inc=1, device_id={"tensor": left}, device_id_type=MESH)

    @pl.when(t < 3)
    def _():
        pl.semaphore_signal(barrier, inc=1, device_id={"tensor": right}, device_id_type=MESH)

    small = (
        pltpu.make_async_copy(seg_hbm, seg_ref, small_sem.at[0]),
        pltpu.make_async_copy(dest_hbm, dest_ref, small_sem.at[1]),
    )
    for copy in small:
        copy.start()
    for copy in loads(0):
        copy.start()
    @pl.when((t == 0) | (t == 3))
    def _():
        pl.semaphore_wait(barrier, 1)

    @pl.when((t == 1) | (t == 2))
    def _():
        pl.semaphore_wait(barrier, 2)

    for c in range(KEYS):
        for part, i in ((1, 0), (0, 0), (1, 1), (0, 1)):
            @pl.when(sends[part])
            def _():
                remote(c, part, (i,))[0].start()

    for c in range(1, KEYS):
        for copy in loads(c):
            copy.start()
    for part in range(2):
        rows = slice(part * BLOCK, (part + 1) * BLOCK)

        @pl.when(jnp.logical_not(receives[part]))
        def _():
            k_s[:, rows, :] = jnp.zeros((KEYS, BLOCK, HEAD), jnp.bfloat16)
            v_s[:, rows, :] = jnp.zeros((KEYS, BLOCK, HEAD), jnp.bfloat16)

        @pl.when(jnp.logical_not(sends[part]))
        def _():
            k_in[:, rows, :] = jnp.zeros((KEYS, BLOCK, HEAD), jnp.bfloat16)
            v_in[:, rows, :] = jnp.zeros((KEYS, BLOCK, HEAD), jnp.bfloat16)

    for copy in small:
        copy.wait()
    for b in range(3):
        block = 3 * t + b
        pack = block // 4
        segs = seg_ref[pl.ds(pack, 1), :]
        first = jnp.sum((segs == 0).astype(jnp.int32), axis=1, keepdims=True)
        second = jnp.sum((segs <= 1).astype(jnp.int32), axis=1, keepdims=True)
        for sub in range(4):
            base = (block - 4 * pack) * BLOCK + sub * SUB
            row = lax.rem(lax.broadcasted_iota(jnp.int32, (1, 4 * SUB), 1), SUB) + base
            start = jnp.where(row >= second, second, jnp.where(row >= first, first, 0))
            key = lax.broadcasted_iota(jnp.int32, (WINDOW, 4 * SUB), 0) + (base - 256)
            bias_s[b * 4 + sub] = jnp.where((key >= start) & (key <= row), 0.0, MASKED)
    dk_acc[...] = jnp.zeros_like(dk_acc)
    dv_acc[...] = jnp.zeros_like(dv_acc)

    def live_scale(b):
        alive = dest_ref[0, (3 * t + b) // 4] >= 0
        return jnp.where(alive, 1.0, 0.0).astype(jnp.float32)

    def arrived(c):
        for copy in loads(c):
            copy.wait()
        keys_transposed(c, 2, 5)

    def rows_of(b, sub):
        return slice(b * BLOCK + sub * SUB, b * BLOCK + (sub + 1) * SUB)

    def lowest(kind, sub):
        return max(0, (2 - kind) * BLOCK - sub * SUB)

    def window_of(b, sub, low=0):
        return slice(b * BLOCK + sub * SUB + low, b * BLOCK + sub * SUB + WINDOW)

    def stacked(ref, b, sub, c):
        rows = rows_of(b, sub)
        return jnp.concatenate([ref[c, rows, h * HEAD : (h + 1) * HEAD] for h in range(GROUP)], axis=0)

    def products(ref, other, item):
        b, sub, kind, c = item
        return lax.dot_general(
            ref[c, window_of(b, sub, lowest(kind, sub)), :], stacked(other, b, sub, c), (((1,), (1,)), ((), ())),
            preferred_element_type=jnp.float32)

    def scores_of(item, slot):
        low = lowest(item[2], item[1])
        s_buf[slot, low:] = products(k_s, q_s, item)
        dp_buf[slot, low:] = products(v_s, o_s, item)

    def softmax(item, slot, lanes):
        b, sub, kind, c = item
        low = lowest(kind, sub)
        scores = s_buf[slot, low:, lanes] + bias_s[b * 4 + sub, low:]
        top = jnp.max(scores, axis=0, keepdims=True)
        weights = jnp.exp2((scores - top) * exponent)
        return weights * (1.0 / jnp.sum(weights, axis=0, keepdims=True))

    def dscores_of(probs, dprobs):
        delta = jnp.sum(probs * dprobs, axis=0, keepdims=True)
        return (probs * (dprobs - delta)).astype(jnp.bfloat16)

    def softmax_of(item, slot):
        b, sub, kind, c = item
        low = lowest(kind, sub)
        base = BLOCK if kind == FIRST else 0
        if low > base:
            ds_s[slot, base:low] = jnp.zeros((low - base, GROUP * SUB), jnp.bfloat16)
        for i in range(2):
            lanes = slice(i * HEAD, (i + 1) * HEAD)
            probs = softmax(item, slot, lanes)
            p_s[slot, low:, lanes] = probs.astype(jnp.bfloat16)
            ds_s[slot, low:, lanes] = dscores_of(probs, dp_buf[slot, low:, lanes])

    def query_and_key_sums(item, slot):
        b, sub, kind, c = item
        low = lowest(kind, sub)
        if kind == FIRST:
            keys = jnp.concatenate([kt_s[c, sub, b + 1], kt_s[c, sub, b + 2, :, :SUB]], axis=1)
            dq_t = jnp.dot(keys, ds_s[slot, BLOCK:], preferred_element_type=jnp.float32)
        else:
            keys = jnp.concatenate([kt_s[c, sub, b], kt_s[c, sub, b + 1]], axis=1)
            dq_t = jnp.dot(keys, ds_s[slot, : 2 * BLOCK], preferred_element_type=jnp.float32)
            dq_t = dq_t + jnp.dot(
                kt_s[c, sub, b + 2, :, :SUB], ds_s[slot, 2 * BLOCK :], preferred_element_type=jnp.float32)
        dq = (dq_t * (scale * live_scale(b))).astype(jnp.bfloat16).T
        rows = rows_of(b, sub)
        for h in range(GROUP):
            at = pl.multiple_of(c * (GROUP * HEAD) + h * HEAD, HEAD)
            dq_ref[rows, pl.ds(at, HEAD)] = dq[h * SUB : (h + 1) * SUB]
        dk_acc[c, window_of(b, sub, low), :] += jnp.dot(
            ds_s[slot, low:], stacked(q_s, b, sub, c), preferred_element_type=jnp.float32)

    def value_sums(item, half):
        b, sub, kind, c = item
        low = lowest(kind, sub)
        dv_acc[c, window_of(b, sub, low), :] += jnp.dot(
            half[low:], stacked(o_s, b, sub, c), preferred_element_type=jnp.float32)

    def gradients(item, slot):
        query_and_key_sums(item, slot)
        value_sums(item, p_s.at[slot])

    def items_of(b, kind, c):
        return [(b, sub, kind, c) for sub in range(4)]

    def pipeline(items, old=(None, None), drain=False, then=None):
        chain = [*old, *items]
        for k, item in enumerate(items):
            scores_of(item, k % 2)
            if chain[k] is not None:
                gradients(chain[k], k % 2)
                if then is not None and k in then:
                    then[k]()
            if chain[k + 1] is not None:
                softmax_of(chain[k + 1], (k + 1) % 2)
        if drain:
            drain_of(items)

    def drain_of(items):
        gradients(items[-2], 0)
        softmax_of(items[-1], 1)
        gradients(items[-1], 1)

    def keys_transposed(c, first, last):
        for sub in range(4):
            for w in range(first, last):
                at = w * BLOCK + sub * SUB
                if at + BLOCK <= 640:
                    kt_s[c, sub, w] = k_s[c, pl.ds(at, BLOCK), :].T
                else:
                    kt_s[c, sub, w] = jnp.concatenate(
                        [k_s[c, pl.ds(at, 640 - at), :].T, jnp.zeros((HEAD, BLOCK - 640 + at), jnp.bfloat16)], axis=1)

    def remote_arrived(c, which):
        for part in range(2):
            @pl.when(receives[part])
            def _():
                for i in which:
                    remote(c, part)[i].wait_recv()

        if 0 in which:
            keys_transposed(c, 0, 2)

    def phase_one(blocks, c, then=None):
        items = [item for b in blocks for item in items_of(b, LATER, c)]
        for k in range(len(items) + 2):
            if k < len(items):
                s_buf[k % 2] = products(k_s, q_s, items[k])
            if k >= 2:
                value_sums(items[k - 2], p_half.at[k - 2])
            if 1 <= k < len(items) + 1:
                for i in range(2):
                    lanes = slice(i * HEAD, (i + 1) * HEAD)
                    probs = softmax(items[k - 1], (k - 1) % 2, lanes)
                    p_full[k - 1, :, lanes] = probs
                    p_half[k - 1, :, lanes] = probs.astype(jnp.bfloat16)
            if then is not None and k in then:
                then[k]()

    def phase_two(blocks, c, then=None):
        items = [item for b in blocks for item in items_of(b, LATER, c)]
        for k in range(len(items) + 2):
            if k < len(items):
                dp_buf[k % 2] = products(v_s, o_s, items[k])
            if k >= 2:
                query_and_key_sums(items[k - 2], k % 2)
            if 1 <= k < len(items) + 1:
                for i in range(2):
                    lanes = slice(i * HEAD, (i + 1) * HEAD)
                    ds_s[(k - 1) % 2, :, lanes] = dscores_of(
                        p_full[k - 1, :, lanes], dp_buf[(k - 1) % 2, :, lanes])
            if then is not None and k in then:
                then[k]()

    def wait_for(c, part, which=(0, 1)):
        for copy in remote(c, part, which):
            copy.wait_recv()

    def loop(first, last):
        def run(body):
            def step(c, carry):
                body(c)
                return carry

            lax.fori_loop(first, last, step, 0)

        return run

    last = KEYS - 1

    @pl.when(t == 0)
    def _():
        @loop(0, KEYS)
        def _(c):
            arrived(c)
            keys_transposed(c, 1, 2)
            pipeline(items_of(0, FIRST, c) + items_of(1, SECOND, c) + items_of(2, LATER, c), drain=True)

    @pl.when(t == 1)
    def _():
        def own(c):
            arrived(c)
            pipeline(items_of(1, FIRST, c) + items_of(2, SECOND, c), drain=True)

        loop(0, 2)(own)

        @loop(0, KEYS)
        def _(c):
            wait_for(c, 1, (0,))
            wait_for(c, 0, (0,))
            keys_transposed(c, 0, 2)
            phase_one((0,), c)
            send_back(c, 0, (1,))
            send_back(c, 1, (1,))
            wait_for(c, 1, (1,))
            wait_for(c, 0, (1,))
            phase_two((0,), c)
            send_back(c, 0, (0,))
            send_back(c, 1, (0,))

            @pl.when(c < 2)
            def _():
                own(c + 2)

    @pl.when(t == 2)
    def _():
        @loop(0, KEYS)
        def _(c):
            arrived(c)
            pipeline(items_of(2, FIRST, c), drain=True)

        @loop(0, KEYS)
        def _(c):
            at_ends = (c == 0) | (c == last)

            @pl.when(at_ends)
            def _():
                wait_for(c, 1, (0,))
                wait_for(c, 0, (0,))
                keys_transposed(c, 0, 2)
                phase_one((0, 1), c, {5: lambda: send_back(c, 0, (1,))})
                send_back(c, 1, (1,))
                wait_for(c, 1, (1,))
                wait_for(c, 0, (1,))
                phase_two((0, 1), c, {5: lambda: send_back(c, 0, (0,))})
                send_back(c, 1, (0,))

            @pl.when(jnp.logical_not(at_ends))
            def _():
                wait_for(c, 1)
                wait_for(c, 0)
                keys_transposed(c, 0, 2)
                pipeline(
                    items_of(0, LATER, c) + items_of(1, LATER, c), drain=True,
                    then={5: lambda: send_back(c, 0, (0, 1))})
                send_back(c, 1, (0, 1))

    @pl.when(t == 3)
    def _():
        def own(c, old=(None, None), drain=False):
            pipeline(items_of(2, LATER, c), old, drain)

        def shared(c, old):
            wait_for(c, 1)
            keys_transposed(c, 0, 2)
            pipeline(items_of(0, SECOND, c) + items_of(1, LATER, c), old)

        arrived(0)
        own(0)

        @loop(1, last)
        def _(c):
            arrived(c)
            own(c, items_of(2, LATER, c - 1)[2:])

        arrived(last)
        shared(0, items_of(2, LATER, last - 1)[2:])

        @loop(1, KEYS)
        def _(c):
            shared(c, items_of(1, LATER, c - 1)[2:])
            send_back(c - 1, 1, (0, 1))

        drain_of(items_of(1, LATER, last))
        send_back(last, 1, (0, 1))
        own(last, drain=True)

    def result(c, b):
        rows = pl.ds((b + 2) * BLOCK, BLOCK)
        dk = dk_acc[c, rows, :] * scale
        dv = dv_acc[c, rows, :]
        if b:
            dk = dk + k_in[c, pl.ds((b - 1) * BLOCK, BLOCK), :].astype(jnp.float32)
            dv = dv + v_in[c, pl.ds((b - 1) * BLOCK, BLOCK), :].astype(jnp.float32)
        alive = live_scale(b)
        dk_ref[b * BLOCK : (b + 1) * BLOCK, c * HEAD : (c + 1) * HEAD] = (dk * alive).astype(jnp.bfloat16)
        dv_ref[b * BLOCK : (b + 1) * BLOCK, c * HEAD : (c + 1) * HEAD] = (dv * alive).astype(jnp.bfloat16)

    for c in range(KEYS):
        result(c, 0)
    for c in range(KEYS):
        for part in range(2):
            @pl.when(sends[part])
            def _():
                for copy in back(c, part):
                    copy.wait_recv()

            result(c, part + 1)

    for c in range(KEYS):
        for part in range(2):
            @pl.when(receives[part])
            def _():
                for copy in back(c, part):
                    copy.wait_send()

            @pl.when(sends[part])
            def _():
                for copy in remote(c, part):
                    copy.wait_send()


def write_out(q_in, k_in, v_in, q_out, k_out, v_out, sem):
    copies = []
    for i in range(4):
        rows = pl.ds(96 * i, 96)
        copies.append(pltpu.make_async_copy(q_in.at[rows], q_out.at[rows], sem.at[i]))
    copies.append(pltpu.make_async_copy(k_in, k_out, sem.at[4]))
    copies.append(pltpu.make_async_copy(v_in, v_out, sem.at[5]))
    for copy in copies:
        copy.start()
    for copy in copies:
        copy.wait()


def local(queries, key_matrix, value_matrix, out_grads, seg_ids, bucket_dest):
    half, full = jnp.bfloat16, jnp.float32
    rows, q_width = queries.shape
    kv_width = key_matrix.shape[1]
    parts = pl.pallas_call(
        kernel,
        out_shape=(
            pltpu.VMEM((rows, q_width), half),
            pltpu.VMEM((rows, kv_width), half),
            pltpu.VMEM((rows, kv_width), half),
        ),
        in_specs=[pl.BlockSpec(memory_space=pltpu.HBM)] * 6,
        out_specs=[pl.BlockSpec(memory_space=pltpu.VMEM)] * 3,
        scratch_shapes=[
            pltpu.VMEM((KEYS, rows, GROUP * HEAD), half),
            pltpu.VMEM((KEYS, rows, GROUP * HEAD), half),
            pltpu.VMEM((KEYS, rows + 256, HEAD), half),
            pltpu.VMEM((KEYS, rows + 256, HEAD), half),
            pltpu.VMEM((KEYS, 4, 5, HEAD, BLOCK), half),
            pltpu.VMEM((12, WINDOW, 4 * SUB), full),
            pltpu.VMEM((2, WINDOW, GROUP * SUB), full),
            pltpu.VMEM((2, WINDOW, GROUP * SUB), full),
            pltpu.VMEM((2, WINDOW, GROUP * SUB), half),
            pltpu.VMEM((2, WINDOW, GROUP * SUB), half),
            pltpu.VMEM((8, WINDOW, GROUP * SUB), full),
            pltpu.VMEM((8, WINDOW, GROUP * SUB), half),
            pltpu.VMEM((KEYS, rows + 256, HEAD), full),
            pltpu.VMEM((KEYS, rows + 256, HEAD), full),
            pltpu.VMEM((KEYS, 256, HEAD), half),
            pltpu.VMEM((KEYS, 256, HEAD), half),
            pltpu.VMEM((KEYS, 256, HEAD), half),
            pltpu.VMEM((KEYS, 256, HEAD), half),
            pltpu.VMEM((3, 512), jnp.int32),
            pltpu.SMEM((1, 3), jnp.int32),
            pltpu.SemaphoreType.DMA((KEYS, 4)),
            pltpu.SemaphoreType.DMA((2,)),
            pltpu.SemaphoreType.DMA((KEYS, 2, 2)),
            pltpu.SemaphoreType.DMA((KEYS, 2, 2)),
            pltpu.SemaphoreType.DMA((KEYS, 2, 2)),
            pltpu.SemaphoreType.DMA((KEYS, 2, 2)),
        ],
        compiler_params=pltpu.CompilerParams(
            collective_id=0, has_side_effects=True, vmem_limit_bytes=32 * 1024 * 1024
        ),
        name="packed_attention_backward",
    )(
        *[
            pltpu.with_memory_space_constraint(x, pltpu.HBM)
            for x in (queries, key_matrix, value_matrix, out_grads, seg_ids, bucket_dest)
        ]
    )
    return pl.pallas_call(
        write_out,
        out_shape=(
            jax.ShapeDtypeStruct((rows, q_width), half),
            jax.ShapeDtypeStruct((rows, kv_width), half),
            jax.ShapeDtypeStruct((rows, kv_width), half),
        ),
        in_specs=[pl.BlockSpec(memory_space=pltpu.VMEM)] * 3,
        out_specs=[pl.BlockSpec(memory_space=pltpu.HBM)] * 3,
        scratch_shapes=[pltpu.SemaphoreType.DMA((6,))],
        compiler_params=pltpu.CompilerParams(vmem_limit_bytes=4 * 1024 * 1024),
        name="write_out",
    )(*[pltpu.with_memory_space_constraint(p, pltpu.VMEM) for p in parts])


def solution(mesh):
    in_specs = (
        P(("dp", "tensor"), None),
        P(("dp", "tensor"), None),
        P(("dp", "tensor"), None),
        P(("dp", "tensor"), None),
        P("dp", None),
        P("dp", None),
    )
    out_specs = (P(("dp", "tensor"), None), P(("dp", "tensor"), None), P(("dp", "tensor"), None))
    return jax.shard_map(local, mesh=mesh, in_specs=in_specs, out_specs=out_specs, check_vma=False)
```

```python
import math

import jax
import jax.numpy as jnp
from jax import lax
from jax.experimental import pallas as pl
from jax.experimental.pallas import tpu as pltpu
from jax.sharding import PartitionSpec as P

HEAD = 128
GROUP = 8
KEYS = 4
BLOCK = 128
FIRST, SECOND, LATER, BORROWED = 0, 1, 2, 3
SUB = 32
WINDOW = 256 + SUB
MASKED = -1e30
MESH = pl.DeviceIdType.MESH


def kernel(
    q_hbm, k_hbm, v_hbm, o_hbm, seg_hbm, dest_hbm,
    dq_ref, dk_ref, dv_ref,
    q_s, o_s, k_s, v_s, kt_s, bias_s, s_buf, dp_buf, p_s, ds_s, p_full, p_half, ds_kept, dk_acc, dv_acc, k_out, v_out, k_in, v_in,
    seg_ref, dest_ref, load_sem, small_sem, send_sem, recv_sem, back_send_sem, back_recv_sem,
):
    t = lax.axis_index("tensor")
    right, left = lax.rem(t + 1, 4), lax.rem(t + 3, 4)
    scale = 1.0 / math.sqrt(HEAD)
    exponent = scale * math.log2(math.e)

    def loads(c):
        wide = pl.ds(c * (GROUP * HEAD), GROUP * HEAD)
        narrow = pl.ds(c * HEAD, HEAD)
        return (
            pltpu.make_async_copy(k_hbm.at[:, narrow], k_s.at[c, pl.ds(256, 384)], load_sem.at[c, 0]),
            pltpu.make_async_copy(v_hbm.at[:, narrow], v_s.at[c, pl.ds(256, 384)], load_sem.at[c, 1]),
            pltpu.make_async_copy(q_hbm.at[:, wide], q_s.at[c], load_sem.at[c, 2]),
            pltpu.make_async_copy(o_hbm.at[:, wide], o_s.at[c], load_sem.at[c, 3]),
        )

    sends = (t < 2, t < 3)
    receives = ((t == 1) | (t == 2), t > 0)

    def remote(c, part, which=(0, 1)):
        narrow = pl.ds(c * HEAD, HEAD)
        there, here = pl.ds((part + 1) * BLOCK, BLOCK), pl.ds(part * BLOCK, BLOCK)
        return [
            pltpu.make_async_remote_copy(
                source.at[there, narrow], target.at[c, here], send_sem.at[c, part, i], recv_sem.at[c, part, i],
                device_id={"tensor": right}, device_id_type=MESH)
            for i, (source, target) in enumerate(((k_hbm, k_s), (v_hbm, v_s))) if i in which
        ]

    def back(c, part, which=(0, 1)):
        rows = pl.ds(part * BLOCK, BLOCK)
        return [
            pltpu.make_async_remote_copy(
                source.at[c, rows], target.at[c, rows], back_send_sem.at[c, part, i], back_recv_sem.at[c, part, i],
                device_id={"tensor": left}, device_id_type=MESH)
            for i, (source, target) in enumerate(((k_out, k_in), (v_out, v_in))) if i in which
        ]

    def send_back(c, part, which):
        rows = pl.ds(part * BLOCK, BLOCK)
        if 0 in which:
            k_out[c, rows, :] = (dk_acc[c, rows, :] * scale).astype(jnp.bfloat16)
        if 1 in which:
            v_out[c, rows, :] = dv_acc[c, rows, :].astype(jnp.bfloat16)
        for copy in back(c, part, which):
            copy.start()

    barrier = pltpu.get_barrier_semaphore()
    @pl.when(t > 0)
    def _():
        pl.semaphore_signal(barrier, inc=1, device_id={"tensor": left}, device_id_type=MESH)

    @pl.when(t < 3)
    def _():
        pl.semaphore_signal(barrier, inc=1, device_id={"tensor": right}, device_id_type=MESH)

    small = (
        pltpu.make_async_copy(seg_hbm, seg_ref, small_sem.at[0]),
        pltpu.make_async_copy(dest_hbm, dest_ref, small_sem.at[1]),
    )
    for copy in small:
        copy.start()
    for copy in loads(0):
        copy.start()
    @pl.when((t == 0) | (t == 3))
    def _():
        pl.semaphore_wait(barrier, 1)

    @pl.when((t == 1) | (t == 2))
    def _():
        pl.semaphore_wait(barrier, 2)

    for c in range(KEYS):
        for part, i in ((1, 0), (0, 0), (1, 1), (0, 1)):
            @pl.when(sends[part])
            def _():
                remote(c, part, (i,))[0].start()

    for c in range(1, KEYS):
        for copy in loads(c):
            copy.start()
    for part in range(2):
        rows = slice(part * BLOCK, (part + 1) * BLOCK)

        @pl.when(jnp.logical_not(receives[part]))
        def _():
            k_s[:, rows, :] = jnp.zeros((KEYS, BLOCK, HEAD), jnp.bfloat16)
            v_s[:, rows, :] = jnp.zeros((KEYS, BLOCK, HEAD), jnp.bfloat16)

        @pl.when(jnp.logical_not(sends[part]))
        def _():
            k_in[:, rows, :] = jnp.zeros((KEYS, BLOCK, HEAD), jnp.bfloat16)
            v_in[:, rows, :] = jnp.zeros((KEYS, BLOCK, HEAD), jnp.bfloat16)

    for copy in small:
        copy.wait()
    for b in range(3):
        block = 3 * t + b
        pack = block // 4
        segs = seg_ref[pl.ds(pack, 1), :]
        first = jnp.sum((segs == 0).astype(jnp.int32), axis=1, keepdims=True)
        second = jnp.sum((segs <= 1).astype(jnp.int32), axis=1, keepdims=True)
        for sub in range(4):
            base = (block - 4 * pack) * BLOCK + sub * SUB
            row = lax.rem(lax.broadcasted_iota(jnp.int32, (1, 4 * SUB), 1), SUB) + base
            start = jnp.where(row >= second, second, jnp.where(row >= first, first, 0))
            key = lax.broadcasted_iota(jnp.int32, (WINDOW, 4 * SUB), 0) + (base - 256)
            bias_s[b * 4 + sub] = jnp.where((key >= start) & (key <= row), 0.0, MASKED)
    dk_acc[...] = jnp.zeros_like(dk_acc)
    dv_acc[...] = jnp.zeros_like(dv_acc)

    def live_scale(b):
        alive = dest_ref[0, (3 * t + b) // 4] >= 0
        return jnp.where(alive, 1.0, 0.0).astype(jnp.float32)

    def arrived(c):
        for copy in loads(c):
            copy.wait()
        keys_transposed(c, 2, 5)

    def rows_of(b, sub):
        return slice(b * BLOCK + sub * SUB, b * BLOCK + (sub + 1) * SUB)

    def lowest(kind, sub):
        return max(0, (2 - kind) * BLOCK - sub * SUB)

    def window_of(b, sub, low=0):
        return slice(b * BLOCK + sub * SUB + low, b * BLOCK + sub * SUB + WINDOW)

    def stacked(ref, b, sub, c):
        rows = rows_of(b, sub)
        return jnp.concatenate([ref[c, rows, h * HEAD : (h + 1) * HEAD] for h in range(GROUP)], axis=0)

    def products(ref, other, item):
        b, sub, kind, c = item
        return lax.dot_general(
            ref[c, window_of(b, sub, lowest(kind, sub)), :], stacked(other, b, sub, c), (((1,), (1,)), ((), ())),
            preferred_element_type=jnp.float32)

    def scores_of(item, slot):
        low = lowest(item[2], item[1])
        s_buf[slot, low:] = products(k_s, q_s, item)
        dp_buf[slot, low:] = products(v_s, o_s, item)

    def softmax(item, slot, lanes):
        b, sub, kind, c = item
        low = lowest(kind, sub)
        scores = s_buf[slot, low:, lanes] + bias_s[b * 4 + sub, low:]
        top = jnp.max(scores, axis=0, keepdims=True)
        weights = jnp.exp2((scores - top) * exponent)
        return weights * (1.0 / jnp.sum(weights, axis=0, keepdims=True))

    def dscores_of(probs, dprobs):
        delta = jnp.sum(probs * dprobs, axis=0, keepdims=True)
        return (probs * (dprobs - delta)).astype(jnp.bfloat16)

    def ds_of(item, slot):
        b, sub, kind, c = item
        return ds_kept.at[c, b * 4 + sub] if kind == BORROWED else ds_s.at[slot]

    def softmax_of(item, slot):
        b, sub, kind, c = item
        low = lowest(kind, sub)
        base = BLOCK if kind == FIRST else 0
        if low > base:
            ds_s[slot, base:low] = jnp.zeros((low - base, GROUP * SUB), jnp.bfloat16)
        ds_ref = ds_of(item, slot)
        for i in range(2):
            lanes = slice(i * HEAD, (i + 1) * HEAD)
            probs = softmax(item, slot, lanes)
            p_s[slot, low:, lanes] = probs.astype(jnp.bfloat16)
            ds_ref[low:, lanes] = dscores_of(probs, dp_buf[slot, low:, lanes])

    def query_gradient(item, ds_ref):
        b, sub, kind, c = item
        if kind == FIRST:
            keys = jnp.concatenate([kt_s[c, sub, b + 1], kt_s[c, sub, b + 2, :, :SUB]], axis=1)
            dq_t = jnp.dot(keys, ds_ref[BLOCK:], preferred_element_type=jnp.float32)
        else:
            keys = jnp.concatenate([kt_s[c, sub, b], kt_s[c, sub, b + 1]], axis=1)
            dq_t = jnp.dot(keys, ds_ref[: 2 * BLOCK], preferred_element_type=jnp.float32)
            dq_t = dq_t + jnp.dot(
                kt_s[c, sub, b + 2, :, :SUB], ds_ref[2 * BLOCK :], preferred_element_type=jnp.float32)
        dq = (dq_t * (scale * live_scale(b))).astype(jnp.bfloat16).T
        rows = rows_of(b, sub)
        for h in range(GROUP):
            at = pl.multiple_of(c * (GROUP * HEAD) + h * HEAD, HEAD)
            dq_ref[rows, pl.ds(at, HEAD)] = dq[h * SUB : (h + 1) * SUB]

    def key_sums(item, ds_ref):
        b, sub, kind, c = item
        low = lowest(kind, sub)
        dk_acc[c, window_of(b, sub, low), :] += jnp.dot(
            ds_ref[low:], stacked(q_s, b, sub, c), preferred_element_type=jnp.float32)

    def value_sums(item, half):
        b, sub, kind, c = item
        low = lowest(kind, sub)
        dv_acc[c, window_of(b, sub, low), :] += jnp.dot(
            half[low:], stacked(o_s, b, sub, c), preferred_element_type=jnp.float32)

    def gradients(item, slot):
        ds_ref = ds_of(item, slot)
        if item[2] != BORROWED:
            query_gradient(item, ds_ref)
        key_sums(item, ds_ref)
        value_sums(item, p_s.at[slot])

    def items_of(b, kind, c):
        return [(b, sub, kind, c) for sub in range(4)]

    def pipeline(items, old=(None, None), drain=False, then=None):
        chain = [*old, *items]
        for k, item in enumerate(items):
            scores_of(item, k % 2)
            if chain[k] is not None:
                gradients(chain[k], k % 2)
                if then is not None and k in then:
                    then[k]()
            if chain[k + 1] is not None:
                softmax_of(chain[k + 1], (k + 1) % 2)
        if drain:
            drain_of(items)

    def drain_of(items):
        gradients(items[-2], 0)
        softmax_of(items[-1], 1)
        gradients(items[-1], 1)

    def keys_transposed(c, first, last):
        for sub in range(4):
            for w in range(first, last):
                at = w * BLOCK + sub * SUB
                if at + BLOCK <= 640:
                    kt_s[c, sub, w] = k_s[c, pl.ds(at, BLOCK), :].T
                else:
                    kt_s[c, sub, w] = jnp.concatenate(
                        [k_s[c, pl.ds(at, 640 - at), :].T, jnp.zeros((HEAD, BLOCK - 640 + at), jnp.bfloat16)], axis=1)

    def remote_arrived(c, which):
        for part in range(2):
            @pl.when(receives[part])
            def _():
                for i in which:
                    remote(c, part)[i].wait_recv()

        if 0 in which:
            keys_transposed(c, 0, 2)

    def phase_one(blocks, c, then=None):
        items = [item for b in blocks for item in items_of(b, BORROWED, c)]
        for k in range(len(items) + 2):
            if k < len(items):
                s_buf[k % 2] = products(k_s, q_s, items[k])
            if k >= 2:
                value_sums(items[k - 2], p_half.at[k - 2])
            if 1 <= k < len(items) + 1:
                for i in range(2):
                    lanes = slice(i * HEAD, (i + 1) * HEAD)
                    probs = softmax(items[k - 1], (k - 1) % 2, lanes)
                    p_full[k - 1, :, lanes] = probs
                    p_half[k - 1, :, lanes] = probs.astype(jnp.bfloat16)
            if then is not None and k in then:
                then[k]()

    def phase_two(blocks, c, then=None):
        items = [item for b in blocks for item in items_of(b, BORROWED, c)]
        for k in range(len(items) + 2):
            if k < len(items):
                dp_buf[k % 2] = products(v_s, o_s, items[k])
            if k >= 2:
                key_sums(items[k - 2], ds_of(items[k - 2], k % 2))
            if 1 <= k < len(items) + 1:
                for i in range(2):
                    lanes = slice(i * HEAD, (i + 1) * HEAD)
                    ds_of(items[k - 1], (k - 1) % 2)[:, lanes] = dscores_of(
                        p_full[k - 1, :, lanes], dp_buf[(k - 1) % 2, :, lanes])
            if then is not None and k in then:
                then[k]()

    def kept_gradients(blocks, c):
        for b in blocks:
            for item in items_of(b, BORROWED, c):
                query_gradient(item, ds_of(item, 0))

    def wait_for(c, part, which=(0, 1)):
        for copy in remote(c, part, which):
            copy.wait_recv()

    def loop(first, last):
        def run(body):
            def step(c, carry):
                body(c)
                return carry

            lax.fori_loop(first, last, step, 0)

        return run

    last = KEYS - 1

    @pl.when(t == 0)
    def _():
        @loop(0, KEYS)
        def _(c):
            arrived(c)
            keys_transposed(c, 1, 2)
            pipeline(items_of(0, FIRST, c) + items_of(1, SECOND, c) + items_of(2, LATER, c), drain=True)

    @pl.when(t == 1)
    def _():
        def own(c):
            arrived(c)
            pipeline(items_of(1, FIRST, c) + items_of(2, SECOND, c), drain=True)

        loop(0, 2)(own)

        @loop(0, KEYS)
        def _(c):
            wait_for(c, 1, (0,))
            wait_for(c, 0, (0,))
            keys_transposed(c, 0, 2)
            phase_one((0,), c)
            send_back(c, 0, (1,))
            send_back(c, 1, (1,))
            wait_for(c, 1, (1,))
            wait_for(c, 0, (1,))
            phase_two((0,), c)
            send_back(c, 0, (0,))
            send_back(c, 1, (0,))

            @pl.when(c < 2)
            def _():
                own(c + 2)

        @loop(0, KEYS)
        def _(c):
            kept_gradients((0,), c)

    @pl.when(t == 2)
    def _():
        @loop(0, KEYS)
        def _(c):
            arrived(c)
            pipeline(items_of(2, FIRST, c), drain=True)

        @loop(0, KEYS)
        def _(c):
            at_ends = (c == 0) | (c == last)

            @pl.when(at_ends)
            def _():
                wait_for(c, 1, (0,))
                wait_for(c, 0, (0,))
                keys_transposed(c, 0, 2)
                phase_one((0, 1), c, {5: lambda: send_back(c, 0, (1,))})
                send_back(c, 1, (1,))
                wait_for(c, 1, (1,))
                wait_for(c, 0, (1,))
                phase_two((0, 1), c, {5: lambda: send_back(c, 0, (0,))})
                send_back(c, 1, (0,))

            @pl.when(jnp.logical_not(at_ends))
            def _():
                wait_for(c, 1)
                wait_for(c, 0)
                keys_transposed(c, 0, 2)
                pipeline(
                    items_of(0, BORROWED, c) + items_of(1, BORROWED, c), drain=True,
                    then={5: lambda: send_back(c, 0, (0, 1))})
                send_back(c, 1, (0, 1))

        @loop(0, KEYS)
        def _(c):
            kept_gradients((0, 1), c)

    @pl.when(t == 3)
    def _():
        def own(c, old=(None, None), drain=False):
            pipeline(items_of(2, LATER, c), old, drain)

        def shared(c, old):
            wait_for(c, 1)
            keys_transposed(c, 0, 2)
            pipeline(items_of(0, SECOND, c) + items_of(1, LATER, c), old)

        arrived(0)
        own(0)

        @loop(1, last)
        def _(c):
            arrived(c)
            own(c, items_of(2, LATER, c - 1)[2:])

        arrived(last)
        shared(0, items_of(2, LATER, last - 1)[2:])

        @loop(1, KEYS)
        def _(c):
            shared(c, items_of(1, LATER, c - 1)[2:])
            send_back(c - 1, 1, (0, 1))

        drain_of(items_of(1, LATER, last))
        send_back(last, 1, (0, 1))
        own(last, drain=True)

    def result(c, b):
        rows = pl.ds((b + 2) * BLOCK, BLOCK)
        dk = dk_acc[c, rows, :] * scale
        dv = dv_acc[c, rows, :]
        if b:
            dk = dk + k_in[c, pl.ds((b - 1) * BLOCK, BLOCK), :].astype(jnp.float32)
            dv = dv + v_in[c, pl.ds((b - 1) * BLOCK, BLOCK), :].astype(jnp.float32)
        alive = live_scale(b)
        dk_ref[b * BLOCK : (b + 1) * BLOCK, c * HEAD : (c + 1) * HEAD] = (dk * alive).astype(jnp.bfloat16)
        dv_ref[b * BLOCK : (b + 1) * BLOCK, c * HEAD : (c + 1) * HEAD] = (dv * alive).astype(jnp.bfloat16)

    for c in range(KEYS):
        result(c, 0)
    for c in range(KEYS):
        for part in range(2):
            @pl.when(sends[part])
            def _():
                for copy in back(c, part):
                    copy.wait_recv()

            result(c, part + 1)

    for c in range(KEYS):
        for part in range(2):
            @pl.when(receives[part])
            def _():
                for copy in back(c, part):
                    copy.wait_send()

            @pl.when(sends[part])
            def _():
                for copy in remote(c, part):
                    copy.wait_send()


def write_out(q_in, k_in, v_in, q_out, k_out, v_out, sem):
    copies = []
    for i in range(4):
        rows = pl.ds(96 * i, 96)
        copies.append(pltpu.make_async_copy(q_in.at[rows], q_out.at[rows], sem.at[i]))
    copies.append(pltpu.make_async_copy(k_in, k_out, sem.at[4]))
    copies.append(pltpu.make_async_copy(v_in, v_out, sem.at[5]))
    for copy in copies:
        copy.start()
    for copy in copies:
        copy.wait()


def local(queries, key_matrix, value_matrix, out_grads, seg_ids, bucket_dest):
    half, full = jnp.bfloat16, jnp.float32
    rows, q_width = queries.shape
    kv_width = key_matrix.shape[1]
    parts = pl.pallas_call(
        kernel,
        out_shape=(
            pltpu.VMEM((rows, q_width), half),
            pltpu.VMEM((rows, kv_width), half),
            pltpu.VMEM((rows, kv_width), half),
        ),
        in_specs=[pl.BlockSpec(memory_space=pltpu.HBM)] * 6,
        out_specs=[pl.BlockSpec(memory_space=pltpu.VMEM)] * 3,
        scratch_shapes=[
            pltpu.VMEM((KEYS, rows, GROUP * HEAD), half),
            pltpu.VMEM((KEYS, rows, GROUP * HEAD), half),
            pltpu.VMEM((KEYS, rows + 256, HEAD), half),
            pltpu.VMEM((KEYS, rows + 256, HEAD), half),
            pltpu.VMEM((KEYS, 4, 5, HEAD, BLOCK), half),
            pltpu.VMEM((12, WINDOW, 4 * SUB), full),
            pltpu.VMEM((2, WINDOW, GROUP * SUB), full),
            pltpu.VMEM((2, WINDOW, GROUP * SUB), full),
            pltpu.VMEM((2, WINDOW, GROUP * SUB), half),
            pltpu.VMEM((2, WINDOW, GROUP * SUB), half),
            pltpu.VMEM((8, WINDOW, GROUP * SUB), full),
            pltpu.VMEM((8, WINDOW, GROUP * SUB), half),
            pltpu.VMEM((KEYS, 8, WINDOW, GROUP * SUB), half),
            pltpu.VMEM((KEYS, rows + 256, HEAD), full),
            pltpu.VMEM((KEYS, rows + 256, HEAD), full),
            pltpu.VMEM((KEYS, 256, HEAD), half),
            pltpu.VMEM((KEYS, 256, HEAD), half),
            pltpu.VMEM((KEYS, 256, HEAD), half),
            pltpu.VMEM((KEYS, 256, HEAD), half),
            pltpu.VMEM((3, 512), jnp.int32),
            pltpu.SMEM((1, 3), jnp.int32),
            pltpu.SemaphoreType.DMA((KEYS, 4)),
            pltpu.SemaphoreType.DMA((2,)),
            pltpu.SemaphoreType.DMA((KEYS, 2, 2)),
            pltpu.SemaphoreType.DMA((KEYS, 2, 2)),
            pltpu.SemaphoreType.DMA((KEYS, 2, 2)),
            pltpu.SemaphoreType.DMA((KEYS, 2, 2)),
        ],
        compiler_params=pltpu.CompilerParams(
            collective_id=0, has_side_effects=True, vmem_limit_bytes=32 * 1024 * 1024
        ),
        name="packed_attention_backward",
    )(
        *[
            pltpu.with_memory_space_constraint(x, pltpu.HBM)
            for x in (queries, key_matrix, value_matrix, out_grads, seg_ids, bucket_dest)
        ]
    )
    return pl.pallas_call(
        write_out,
        out_shape=(
            jax.ShapeDtypeStruct((rows, q_width), half),
            jax.ShapeDtypeStruct((rows, kv_width), half),
            jax.ShapeDtypeStruct((rows, kv_width), half),
        ),
        in_specs=[pl.BlockSpec(memory_space=pltpu.VMEM)] * 3,
        out_specs=[pl.BlockSpec(memory_space=pltpu.HBM)] * 3,
        scratch_shapes=[pltpu.SemaphoreType.DMA((6,))],
        compiler_params=pltpu.CompilerParams(vmem_limit_bytes=4 * 1024 * 1024),
        name="write_out",
    )(*[pltpu.with_memory_space_constraint(p, pltpu.VMEM) for p in parts])


def solution(mesh):
    in_specs = (
        P(("dp", "tensor"), None),
        P(("dp", "tensor"), None),
        P(("dp", "tensor"), None),
        P(("dp", "tensor"), None),
        P("dp", None),
        P("dp", None),
    )
    out_specs = (P(("dp", "tensor"), None), P(("dp", "tensor"), None), P(("dp", "tensor"), None))
    return jax.shard_map(local, mesh=mesh, in_specs=in_specs, out_specs=out_specs, check_vma=False)
```

```python
import math

import jax
import jax.numpy as jnp
from jax import lax
from jax.experimental import pallas as pl
from jax.experimental.pallas import tpu as pltpu
from jax.sharding import PartitionSpec as P

HEAD = 128
GROUP = 8
KEYS = 4
BLOCK = 128
FIRST, SECOND, LATER, BORROWED = 0, 1, 2, 3
SUB = 32
WINDOW = 256 + SUB
MASKED = -1e30
MESH = pl.DeviceIdType.MESH


def kernel(
    q_hbm, k_hbm, v_hbm, o_hbm, seg_hbm, dest_hbm,
    dq_ref, dk_ref, dv_ref,
    q_s, o_s, k_s, v_s, kt_s, bias_s, s_buf, dp_buf, p_s, ds_s, p_full, p_half, ds_kept, dk_acc, dv_acc, k_out, v_out, k_in, v_in,
    seg_ref, dest_ref, load_sem, small_sem, send_sem, recv_sem, back_send_sem, back_recv_sem,
):
    t = lax.axis_index("tensor")
    right, left = lax.rem(t + 1, 4), lax.rem(t + 3, 4)
    scale = 1.0 / math.sqrt(HEAD)
    exponent = scale * math.log2(math.e)

    def loads(c):
        wide = pl.ds(c * (GROUP * HEAD), GROUP * HEAD)
        narrow = pl.ds(c * HEAD, HEAD)
        return (
            pltpu.make_async_copy(k_hbm.at[:, narrow], k_s.at[c, pl.ds(256, 384)], load_sem.at[c, 0]),
            pltpu.make_async_copy(v_hbm.at[:, narrow], v_s.at[c, pl.ds(256, 384)], load_sem.at[c, 1]),
            pltpu.make_async_copy(q_hbm.at[:, wide], q_s.at[c], load_sem.at[c, 2]),
            pltpu.make_async_copy(o_hbm.at[:, wide], o_s.at[c], load_sem.at[c, 3]),
        )

    sends = (t < 2, t < 3)
    receives = ((t == 1) | (t == 2), t > 0)

    def remote(c, part, which=(0, 1)):
        narrow = pl.ds(c * HEAD, HEAD)
        there, here = pl.ds((part + 1) * BLOCK, BLOCK), pl.ds(part * BLOCK, BLOCK)
        return [
            pltpu.make_async_remote_copy(
                source.at[there, narrow], target.at[c, here], send_sem.at[c, part, i], recv_sem.at[c, part, i],
                device_id={"tensor": right}, device_id_type=MESH)
            for i, (source, target) in enumerate(((k_hbm, k_s), (v_hbm, v_s))) if i in which
        ]

    pieces = ((0, BLOCK), (BLOCK, BLOCK // 2), (BLOCK + BLOCK // 2, BLOCK // 2))
    pieces_of = ((0,), (1, 2))

    def back(c, piece, which=(0, 1)):
        rows = pl.ds(*pieces[piece])
        return [
            pltpu.make_async_remote_copy(
                source.at[c, rows], target.at[c, rows], back_send_sem.at[c, piece, i], back_recv_sem.at[c, piece, i],
                device_id={"tensor": left}, device_id_type=MESH)
            for i, (source, target) in enumerate(((k_out, k_in), (v_out, v_in))) if i in which
        ]

    def send_piece(c, piece, which):
        rows = pl.ds(*pieces[piece])
        if 0 in which:
            k_out[c, rows, :] = (dk_acc[c, rows, :] * scale).astype(jnp.bfloat16)
        if 1 in which:
            v_out[c, rows, :] = dv_acc[c, rows, :].astype(jnp.bfloat16)
        for copy in back(c, piece, which):
            copy.start()

    def send_back(c, part, which):
        for piece in pieces_of[part]:
            send_piece(c, piece, which)

    barrier = pltpu.get_barrier_semaphore()
    @pl.when(t > 0)
    def _():
        pl.semaphore_signal(barrier, inc=1, device_id={"tensor": left}, device_id_type=MESH)

    @pl.when(t < 3)
    def _():
        pl.semaphore_signal(barrier, inc=1, device_id={"tensor": right}, device_id_type=MESH)

    small = (
        pltpu.make_async_copy(seg_hbm, seg_ref, small_sem.at[0]),
        pltpu.make_async_copy(dest_hbm, dest_ref, small_sem.at[1]),
    )
    for copy in small:
        copy.start()
    for copy in loads(0):
        copy.start()
    @pl.when((t == 0) | (t == 3))
    def _():
        pl.semaphore_wait(barrier, 1)

    @pl.when((t == 1) | (t == 2))
    def _():
        pl.semaphore_wait(barrier, 2)

    for c in range(KEYS):
        for part, i in ((1, 0), (0, 0), (1, 1), (0, 1)):
            @pl.when(sends[part])
            def _():
                remote(c, part, (i,))[0].start()

    for c in range(1, KEYS):
        for copy in loads(c):
            copy.start()
    for part in range(2):
        rows = slice(part * BLOCK, (part + 1) * BLOCK)

        @pl.when(jnp.logical_not(receives[part]))
        def _():
            k_s[:, rows, :] = jnp.zeros((KEYS, BLOCK, HEAD), jnp.bfloat16)
            v_s[:, rows, :] = jnp.zeros((KEYS, BLOCK, HEAD), jnp.bfloat16)

        @pl.when(jnp.logical_not(sends[part]))
        def _():
            k_in[:, rows, :] = jnp.zeros((KEYS, BLOCK, HEAD), jnp.bfloat16)
            v_in[:, rows, :] = jnp.zeros((KEYS, BLOCK, HEAD), jnp.bfloat16)

    for copy in small:
        copy.wait()
    for b in range(3):
        block = 3 * t + b
        pack = block // 4
        segs = seg_ref[pl.ds(pack, 1), :]
        first = jnp.sum((segs == 0).astype(jnp.int32), axis=1, keepdims=True)
        second = jnp.sum((segs <= 1).astype(jnp.int32), axis=1, keepdims=True)
        for sub in range(4):
            base = (block - 4 * pack) * BLOCK + sub * SUB
            row = lax.rem(lax.broadcasted_iota(jnp.int32, (1, 4 * SUB), 1), SUB) + base
            start = jnp.where(row >= second, second, jnp.where(row >= first, first, 0))
            key = lax.broadcasted_iota(jnp.int32, (WINDOW, 4 * SUB), 0) + (base - 256)
            bias_s[b * 4 + sub] = jnp.where((key >= start) & (key <= row), 0.0, MASKED)
    dk_acc[...] = jnp.zeros_like(dk_acc)
    dv_acc[...] = jnp.zeros_like(dv_acc)

    def live_scale(b):
        alive = dest_ref[0, (3 * t + b) // 4] >= 0
        return jnp.where(alive, 1.0, 0.0).astype(jnp.float32)

    def arrived(c):
        for copy in loads(c):
            copy.wait()
        keys_transposed(c, 2, 5)

    def rows_of(b, sub):
        return slice(b * BLOCK + sub * SUB, b * BLOCK + (sub + 1) * SUB)

    def lowest(kind, sub):
        return max(0, (2 - kind) * BLOCK - sub * SUB)

    def window_of(b, sub, low=0):
        return slice(b * BLOCK + sub * SUB + low, b * BLOCK + sub * SUB + WINDOW)

    def stacked(ref, b, sub, c):
        rows = rows_of(b, sub)
        return jnp.concatenate([ref[c, rows, h * HEAD : (h + 1) * HEAD] for h in range(GROUP)], axis=0)

    def products(ref, other, item):
        b, sub, kind, c = item
        return lax.dot_general(
            ref[c, window_of(b, sub, lowest(kind, sub)), :], stacked(other, b, sub, c), (((1,), (1,)), ((), ())),
            preferred_element_type=jnp.float32)

    def scores_of(item, slot):
        low = lowest(item[2], item[1])
        s_buf[slot, low:] = products(k_s, q_s, item)
        dp_buf[slot, low:] = products(v_s, o_s, item)

    def softmax(item, slot, lanes):
        b, sub, kind, c = item
        low = lowest(kind, sub)
        scores = s_buf[slot, low:, lanes] + bias_s[b * 4 + sub, low:]
        top = jnp.max(scores, axis=0, keepdims=True)
        weights = jnp.exp2((scores - top) * exponent)
        return weights * (1.0 / jnp.sum(weights, axis=0, keepdims=True))

    def dscores_of(probs, dprobs):
        delta = jnp.sum(probs * dprobs, axis=0, keepdims=True)
        return (probs * (dprobs - delta)).astype(jnp.bfloat16)

    def ds_of(item, slot):
        b, sub, kind, c = item
        return ds_kept.at[c, b * 4 + sub] if kind == BORROWED else ds_s.at[slot]

    def softmax_of(item, slot):
        b, sub, kind, c = item
        low = lowest(kind, sub)
        base = BLOCK if kind == FIRST else 0
        if low > base:
            ds_s[slot, base:low] = jnp.zeros((low - base, GROUP * SUB), jnp.bfloat16)
        ds_ref = ds_of(item, slot)
        for i in range(2):
            lanes = slice(i * HEAD, (i + 1) * HEAD)
            probs = softmax(item, slot, lanes)
            p_s[slot, low:, lanes] = probs.astype(jnp.bfloat16)
            ds_ref[low:, lanes] = dscores_of(probs, dp_buf[slot, low:, lanes])

    def query_gradient(item, ds_ref):
        b, sub, kind, c = item
        if kind == FIRST:
            keys = jnp.concatenate([kt_s[c, sub, b + 1], kt_s[c, sub, b + 2, :, :SUB]], axis=1)
            dq_t = jnp.dot(keys, ds_ref[BLOCK:], preferred_element_type=jnp.float32)
        else:
            keys = jnp.concatenate([kt_s[c, sub, b], kt_s[c, sub, b + 1]], axis=1)
            dq_t = jnp.dot(keys, ds_ref[: 2 * BLOCK], preferred_element_type=jnp.float32)
            dq_t = dq_t + jnp.dot(
                kt_s[c, sub, b + 2, :, :SUB], ds_ref[2 * BLOCK :], preferred_element_type=jnp.float32)
        dq = (dq_t * (scale * live_scale(b))).astype(jnp.bfloat16).T
        rows = rows_of(b, sub)
        for h in range(GROUP):
            at = pl.multiple_of(c * (GROUP * HEAD) + h * HEAD, HEAD)
            dq_ref[rows, pl.ds(at, HEAD)] = dq[h * SUB : (h + 1) * SUB]

    def key_sums(item, ds_ref):
        b, sub, kind, c = item
        low = lowest(kind, sub)
        dk_acc[c, window_of(b, sub, low), :] += jnp.dot(
            ds_ref[low:], stacked(q_s, b, sub, c), preferred_element_type=jnp.float32)

    def value_sums(item, half):
        b, sub, kind, c = item
        low = lowest(kind, sub)
        dv_acc[c, window_of(b, sub, low), :] += jnp.dot(
            half[low:], stacked(o_s, b, sub, c), preferred_element_type=jnp.float32)

    def gradients(item, slot):
        ds_ref = ds_of(item, slot)
        if item[2] != BORROWED:
            query_gradient(item, ds_ref)
        key_sums(item, ds_ref)
        value_sums(item, p_s.at[slot])

    def items_of(b, kind, c):
        return [(b, sub, kind, c) for sub in range(4)]

    def pipeline(items, old=(None, None), drain=False):
        chain = [*old, *items]
        for k, item in enumerate(items):
            scores_of(item, k % 2)
            if chain[k] is not None:
                gradients(chain[k], k % 2)
            if chain[k + 1] is not None:
                softmax_of(chain[k + 1], (k + 1) % 2)
        if drain:
            drain_of(items)

    def drain_of(items):
        gradients(items[-2], 0)
        softmax_of(items[-1], 1)
        gradients(items[-1], 1)

    def keys_transposed(c, first, last):
        for sub in range(4):
            for w in range(first, last):
                at = w * BLOCK + sub * SUB
                if at + BLOCK <= 640:
                    kt_s[c, sub, w] = k_s[c, pl.ds(at, BLOCK), :].T
                else:
                    kt_s[c, sub, w] = jnp.concatenate(
                        [k_s[c, pl.ds(at, 640 - at), :].T, jnp.zeros((HEAD, BLOCK - 640 + at), jnp.bfloat16)], axis=1)

    def remote_arrived(c, which):
        for part in range(2):
            @pl.when(receives[part])
            def _():
                for i in which:
                    remote(c, part)[i].wait_recv()

        if 0 in which:
            keys_transposed(c, 0, 2)

    def phase_one(blocks, c, then=None):
        items = [item for b in blocks for item in items_of(b, BORROWED, c)]
        for k in range(len(items) + 2):
            if k < len(items):
                s_buf[k % 2] = products(k_s, q_s, items[k])
            if k >= 2:
                value_sums(items[k - 2], p_half.at[k - 2])
            if 1 <= k < len(items) + 1:
                for i in range(2):
                    lanes = slice(i * HEAD, (i + 1) * HEAD)
                    probs = softmax(items[k - 1], (k - 1) % 2, lanes)
                    p_full[k - 1, :, lanes] = probs
                    p_half[k - 1, :, lanes] = probs.astype(jnp.bfloat16)
            if then is not None and k in then:
                then[k]()

    def phase_two(blocks, c, then=None):
        items = [item for b in blocks for item in items_of(b, BORROWED, c)]
        for k in range(len(items) + 2):
            if k < len(items):
                dp_buf[k % 2] = products(v_s, o_s, items[k])
            if k >= 2:
                key_sums(items[k - 2], ds_of(items[k - 2], k % 2))
            if 1 <= k < len(items) + 1:
                for i in range(2):
                    lanes = slice(i * HEAD, (i + 1) * HEAD)
                    ds_of(items[k - 1], (k - 1) % 2)[:, lanes] = dscores_of(
                        p_full[k - 1, :, lanes], dp_buf[(k - 1) % 2, :, lanes])
            if then is not None and k in then:
                then[k]()

    def kept_gradients(blocks, c):
        for b in blocks:
            for item in items_of(b, BORROWED, c):
                query_gradient(item, ds_of(item, 0))

    def wait_for(c, part, which=(0, 1)):
        for copy in remote(c, part, which):
            copy.wait_recv()

    def loop(first, last):
        def run(body):
            def step(c, carry):
                body(c)
                return carry

            lax.fori_loop(first, last, step, 0)

        return run

    last = KEYS - 1

    @pl.when(t == 0)
    def _():
        @loop(0, KEYS)
        def _(c):
            arrived(c)
            keys_transposed(c, 1, 2)
            pipeline(items_of(0, FIRST, c) + items_of(1, SECOND, c) + items_of(2, LATER, c), drain=True)

    @pl.when(t == 1)
    def _():
        def own(c):
            arrived(c)
            pipeline(items_of(1, FIRST, c) + items_of(2, SECOND, c), drain=True)

        loop(0, 2)(own)

        @loop(0, KEYS)
        def _(c):
            wait_for(c, 1, (0,))
            wait_for(c, 0, (0,))
            keys_transposed(c, 0, 2)
            phase_one((0,), c)
            send_back(c, 0, (1,))
            send_back(c, 1, (1,))
            wait_for(c, 1, (1,))
            wait_for(c, 0, (1,))
            phase_two((0,), c)
            send_back(c, 0, (0,))
            send_back(c, 1, (0,))

            @pl.when(c < 2)
            def _():
                own(c + 2)

        @loop(0, KEYS)
        def _(c):
            kept_gradients((0,), c)

    @pl.when(t == 2)
    def _():
        @loop(0, KEYS)
        def _(c):
            arrived(c)
            pipeline(items_of(2, FIRST, c), drain=True)

        @loop(0, KEYS)
        def _(c):
            wait_for(c, 1, (0,))
            wait_for(c, 0, (0,))
            keys_transposed(c, 0, 2)
            phase_one((0, 1), c, {5: lambda: send_back(c, 0, (1,))})
            send_back(c, 1, (1,))
            wait_for(c, 1, (1,))
            wait_for(c, 0, (1,))
            phase_two((0, 1), c, {5: lambda: send_back(c, 0, (0,)), 7: lambda: send_piece(c, 1, (0,))})
            send_piece(c, 2, (0,))

        @loop(0, KEYS)
        def _(c):
            kept_gradients((0, 1), c)

    @pl.when(t == 3)
    def _():
        def own(c, old=(None, None), drain=False):
            pipeline(items_of(2, LATER, c), old, drain)

        def shared(c, old):
            wait_for(c, 1)
            keys_transposed(c, 0, 2)
            pipeline(items_of(0, SECOND, c) + items_of(1, LATER, c), old)

        arrived(0)
        own(0)

        @loop(1, last)
        def _(c):
            arrived(c)
            own(c, items_of(2, LATER, c - 1)[2:])

        arrived(last)
        shared(0, items_of(2, LATER, last - 1)[2:])

        @loop(1, KEYS)
        def _(c):
            shared(c, items_of(1, LATER, c - 1)[2:])
            send_back(c - 1, 1, (0, 1))

        drain_of(items_of(1, LATER, last))
        send_back(last, 1, (0, 1))
        own(last, drain=True)

    def result(c, b):
        rows = pl.ds((b + 2) * BLOCK, BLOCK)
        dk = dk_acc[c, rows, :] * scale
        dv = dv_acc[c, rows, :]
        if b:
            dk = dk + k_in[c, pl.ds((b - 1) * BLOCK, BLOCK), :].astype(jnp.float32)
            dv = dv + v_in[c, pl.ds((b - 1) * BLOCK, BLOCK), :].astype(jnp.float32)
        alive = live_scale(b)
        dk_ref[b * BLOCK : (b + 1) * BLOCK, c * HEAD : (c + 1) * HEAD] = (dk * alive).astype(jnp.bfloat16)
        dv_ref[b * BLOCK : (b + 1) * BLOCK, c * HEAD : (c + 1) * HEAD] = (dv * alive).astype(jnp.bfloat16)

    for c in range(KEYS):
        result(c, 0)
    for c in range(KEYS):
        for part in range(2):
            @pl.when(sends[part])
            def _():
                for piece in pieces_of[part]:
                    for copy in back(c, piece):
                        copy.wait_recv()

            result(c, part + 1)

    for c in range(KEYS):
        for part in range(2):
            @pl.when(receives[part])
            def _():
                for piece in pieces_of[part]:
                    for copy in back(c, piece):
                        copy.wait_send()

            @pl.when(sends[part])
            def _():
                for copy in remote(c, part):
                    copy.wait_send()


def write_out(q_in, k_in, v_in, q_out, k_out, v_out, sem):
    copies = []
    for i in range(4):
        rows = pl.ds(96 * i, 96)
        copies.append(pltpu.make_async_copy(q_in.at[rows], q_out.at[rows], sem.at[i]))
    copies.append(pltpu.make_async_copy(k_in, k_out, sem.at[4]))
    copies.append(pltpu.make_async_copy(v_in, v_out, sem.at[5]))
    for copy in copies:
        copy.start()
    for copy in copies:
        copy.wait()


def local(queries, key_matrix, value_matrix, out_grads, seg_ids, bucket_dest):
    half, full = jnp.bfloat16, jnp.float32
    rows, q_width = queries.shape
    kv_width = key_matrix.shape[1]
    parts = pl.pallas_call(
        kernel,
        out_shape=(
            pltpu.VMEM((rows, q_width), half),
            pltpu.VMEM((rows, kv_width), half),
            pltpu.VMEM((rows, kv_width), half),
        ),
        in_specs=[pl.BlockSpec(memory_space=pltpu.HBM)] * 6,
        out_specs=[pl.BlockSpec(memory_space=pltpu.VMEM)] * 3,
        scratch_shapes=[
            pltpu.VMEM((KEYS, rows, GROUP * HEAD), half),
            pltpu.VMEM((KEYS, rows, GROUP * HEAD), half),
            pltpu.VMEM((KEYS, rows + 256, HEAD), half),
            pltpu.VMEM((KEYS, rows + 256, HEAD), half),
            pltpu.VMEM((KEYS, 4, 5, HEAD, BLOCK), half),
            pltpu.VMEM((12, WINDOW, 4 * SUB), full),
            pltpu.VMEM((2, WINDOW, GROUP * SUB), full),
            pltpu.VMEM((2, WINDOW, GROUP * SUB), full),
            pltpu.VMEM((2, WINDOW, GROUP * SUB), half),
            pltpu.VMEM((2, WINDOW, GROUP * SUB), half),
            pltpu.VMEM((8, WINDOW, GROUP * SUB), full),
            pltpu.VMEM((8, WINDOW, GROUP * SUB), half),
            pltpu.VMEM((KEYS, 8, WINDOW, GROUP * SUB), half),
            pltpu.VMEM((KEYS, rows + 256, HEAD), full),
            pltpu.VMEM((KEYS, rows + 256, HEAD), full),
            pltpu.VMEM((KEYS, 256, HEAD), half),
            pltpu.VMEM((KEYS, 256, HEAD), half),
            pltpu.VMEM((KEYS, 256, HEAD), half),
            pltpu.VMEM((KEYS, 256, HEAD), half),
            pltpu.VMEM((3, 512), jnp.int32),
            pltpu.SMEM((1, 3), jnp.int32),
            pltpu.SemaphoreType.DMA((KEYS, 4)),
            pltpu.SemaphoreType.DMA((2,)),
            pltpu.SemaphoreType.DMA((KEYS, 2, 2)),
            pltpu.SemaphoreType.DMA((KEYS, 2, 2)),
            pltpu.SemaphoreType.DMA((KEYS, 3, 2)),
            pltpu.SemaphoreType.DMA((KEYS, 3, 2)),
        ],
        compiler_params=pltpu.CompilerParams(
            collective_id=0, has_side_effects=True, vmem_limit_bytes=32 * 1024 * 1024
        ),
        name="packed_attention_backward",
    )(
        *[
            pltpu.with_memory_space_constraint(x, pltpu.HBM)
            for x in (queries, key_matrix, value_matrix, out_grads, seg_ids, bucket_dest)
        ]
    )
    return pl.pallas_call(
        write_out,
        out_shape=(
            jax.ShapeDtypeStruct((rows, q_width), half),
            jax.ShapeDtypeStruct((rows, kv_width), half),
            jax.ShapeDtypeStruct((rows, kv_width), half),
        ),
        in_specs=[pl.BlockSpec(memory_space=pltpu.VMEM)] * 3,
        out_specs=[pl.BlockSpec(memory_space=pltpu.HBM)] * 3,
        scratch_shapes=[pltpu.SemaphoreType.DMA((6,))],
        compiler_params=pltpu.CompilerParams(vmem_limit_bytes=4 * 1024 * 1024),
        name="write_out",
    )(*[pltpu.with_memory_space_constraint(p, pltpu.VMEM) for p in parts])


def solution(mesh):
    in_specs = (
        P(("dp", "tensor"), None),
        P(("dp", "tensor"), None),
        P(("dp", "tensor"), None),
        P(("dp", "tensor"), None),
        P("dp", None),
        P("dp", None),
    )
    out_specs = (P(("dp", "tensor"), None), P(("dp", "tensor"), None), P(("dp", "tensor"), None))
    return jax.shard_map(local, mesh=mesh, in_specs=in_specs, out_specs=out_specs, check_vma=False)
```

```python
import math

import jax
import jax.numpy as jnp
from jax import lax
from jax.experimental import pallas as pl
from jax.experimental.pallas import tpu as pltpu
from jax.sharding import PartitionSpec as P

HEAD = 128
GROUP = 8
KEYS = 4
BLOCK = 128
FIRST, SECOND, LATER, BORROWED = 0, 1, 2, 3
SUB = 32
WINDOW = 256 + SUB
MASKED = -1e30
MESH = pl.DeviceIdType.MESH


def kernel(
    q_hbm, k_hbm, v_hbm, o_hbm, seg_hbm, dest_hbm,
    dq_ref, dk_ref, dv_ref,
    q_s, o_s, k_s, v_s, kt_s, bias_s, s_buf, dp_buf, p_s, ds_s, p_full, p_half, ds_kept, dk_acc, dv_acc, k_out, v_out, k_in, v_in,
    seg_ref, dest_ref, load_sem, small_sem, send_sem, recv_sem, back_send_sem, back_recv_sem,
):
    t = lax.axis_index("tensor")
    right, left = lax.rem(t + 1, 4), lax.rem(t + 3, 4)
    scale = 1.0 / math.sqrt(HEAD)
    exponent = scale * math.log2(math.e)

    def loads(c):
        wide = pl.ds(c * (GROUP * HEAD), GROUP * HEAD)
        narrow = pl.ds(c * HEAD, HEAD)
        return (
            pltpu.make_async_copy(k_hbm.at[:, narrow], k_s.at[c, pl.ds(256, 384)], load_sem.at[c, 0]),
            pltpu.make_async_copy(v_hbm.at[:, narrow], v_s.at[c, pl.ds(256, 384)], load_sem.at[c, 1]),
            pltpu.make_async_copy(q_hbm.at[:, wide], q_s.at[c], load_sem.at[c, 2]),
            pltpu.make_async_copy(o_hbm.at[:, wide], o_s.at[c], load_sem.at[c, 3]),
        )

    sends = (t < 2, t < 3)
    receives = ((t == 1) | (t == 2), t > 0)

    def remote(c, part, which=(0, 1)):
        there, here = pl.ds((part + 3) * BLOCK, BLOCK), pl.ds(part * BLOCK, BLOCK)
        return [
            pltpu.make_async_remote_copy(
                target.at[c, there], target.at[c, here], send_sem.at[c, part, i], recv_sem.at[c, part, i],
                device_id={"tensor": right}, device_id_type=MESH)
            for i, target in enumerate((k_s, v_s)) if i in which
        ]

    pieces = ((0, BLOCK), (BLOCK, BLOCK // 2), (BLOCK + BLOCK // 2, BLOCK // 2))
    pieces_of = ((0,), (1, 2))

    def back(c, piece, which=(0, 1)):
        rows = pl.ds(*pieces[piece])
        return [
            pltpu.make_async_remote_copy(
                source.at[c, rows], target.at[c, rows], back_send_sem.at[c, piece, i], back_recv_sem.at[c, piece, i],
                device_id={"tensor": left}, device_id_type=MESH)
            for i, (source, target) in enumerate(((k_out, k_in), (v_out, v_in))) if i in which
        ]

    def send_piece(c, piece, which):
        rows = pl.ds(*pieces[piece])
        if 0 in which:
            k_out[c, rows, :] = (dk_acc[c, rows, :] * scale).astype(jnp.bfloat16)
        if 1 in which:
            v_out[c, rows, :] = dv_acc[c, rows, :].astype(jnp.bfloat16)
        for copy in back(c, piece, which):
            copy.start()

    def send_back(c, part, which):
        for piece in pieces_of[part]:
            send_piece(c, piece, which)

    barrier = pltpu.get_barrier_semaphore()
    @pl.when(t > 0)
    def _():
        pl.semaphore_signal(barrier, inc=1, device_id={"tensor": left}, device_id_type=MESH)

    @pl.when(t < 3)
    def _():
        pl.semaphore_signal(barrier, inc=1, device_id={"tensor": right}, device_id_type=MESH)

    small = (
        pltpu.make_async_copy(seg_hbm, seg_ref, small_sem.at[0]),
        pltpu.make_async_copy(dest_hbm, dest_ref, small_sem.at[1]),
    )
    for copy in small:
        copy.start()
    for c in range(KEYS):
        for copy in loads(c)[:2]:
            copy.start()
    for copy in loads(0)[2:]:
        copy.start()
    @pl.when((t == 0) | (t == 3))
    def _():
        pl.semaphore_wait(barrier, 1)

    @pl.when((t == 1) | (t == 2))
    def _():
        pl.semaphore_wait(barrier, 2)

    for c in range(KEYS):
        for copy in loads(c)[:2]:
            copy.wait()
        for part, i in ((1, 0), (0, 0), (1, 1), (0, 1)):
            @pl.when(sends[part])
            def _():
                remote(c, part, (i,))[0].start()

    for c in range(1, KEYS):
        for copy in loads(c)[2:]:
            copy.start()
    for part in range(2):
        rows = slice(part * BLOCK, (part + 1) * BLOCK)

        @pl.when(jnp.logical_not(receives[part]))
        def _():
            k_s[:, rows, :] = jnp.zeros((KEYS, BLOCK, HEAD), jnp.bfloat16)
            v_s[:, rows, :] = jnp.zeros((KEYS, BLOCK, HEAD), jnp.bfloat16)

        @pl.when(jnp.logical_not(sends[part]))
        def _():
            k_in[:, rows, :] = jnp.zeros((KEYS, BLOCK, HEAD), jnp.bfloat16)
            v_in[:, rows, :] = jnp.zeros((KEYS, BLOCK, HEAD), jnp.bfloat16)

    for copy in small:
        copy.wait()
    for b in range(3):
        block = 3 * t + b
        pack = block // 4
        segs = seg_ref[pl.ds(pack, 1), :]
        first = jnp.sum((segs == 0).astype(jnp.int32), axis=1, keepdims=True)
        second = jnp.sum((segs <= 1).astype(jnp.int32), axis=1, keepdims=True)
        for sub in range(4):
            base = (block - 4 * pack) * BLOCK + sub * SUB
            row = lax.rem(lax.broadcasted_iota(jnp.int32, (1, 4 * SUB), 1), SUB) + base
            start = jnp.where(row >= second, second, jnp.where(row >= first, first, 0))
            key = lax.broadcasted_iota(jnp.int32, (WINDOW, 4 * SUB), 0) + (base - 256)
            bias_s[b * 4 + sub] = jnp.where((key >= start) & (key <= row), 0.0, MASKED)
    dk_acc[...] = jnp.zeros_like(dk_acc)
    dv_acc[...] = jnp.zeros_like(dv_acc)

    def live_scale(b):
        alive = dest_ref[0, (3 * t + b) // 4] >= 0
        return jnp.where(alive, 1.0, 0.0).astype(jnp.float32)

    def arrived(c):
        for copy in loads(c)[2:]:
            copy.wait()
        keys_transposed(c, 2, 5)

    def rows_of(b, sub):
        return slice(b * BLOCK + sub * SUB, b * BLOCK + (sub + 1) * SUB)

    def lowest(kind, sub):
        return max(0, (2 - kind) * BLOCK - sub * SUB)

    def window_of(b, sub, low=0):
        return slice(b * BLOCK + sub * SUB + low, b * BLOCK + sub * SUB + WINDOW)

    def stacked(ref, b, sub, c):
        rows = rows_of(b, sub)
        return jnp.concatenate([ref[c, rows, h * HEAD : (h + 1) * HEAD] for h in range(GROUP)], axis=0)

    def products(ref, other, item):
        b, sub, kind, c = item
        return lax.dot_general(
            ref[c, window_of(b, sub, lowest(kind, sub)), :], stacked(other, b, sub, c), (((1,), (1,)), ((), ())),
            preferred_element_type=jnp.float32)

    def scores_of(item, slot):
        low = lowest(item[2], item[1])
        s_buf[slot, low:] = products(k_s, q_s, item)
        dp_buf[slot, low:] = products(v_s, o_s, item)

    def softmax(item, slot, lanes):
        b, sub, kind, c = item
        low = lowest(kind, sub)
        scores = s_buf[slot, low:, lanes] + bias_s[b * 4 + sub, low:]
        top = jnp.max(scores, axis=0, keepdims=True)
        weights = jnp.exp2((scores - top) * exponent)
        return weights * (1.0 / jnp.sum(weights, axis=0, keepdims=True))

    def dscores_of(probs, dprobs):
        delta = jnp.sum(probs * dprobs, axis=0, keepdims=True)
        return (probs * (dprobs - delta)).astype(jnp.bfloat16)

    def ds_of(item, slot):
        b, sub, kind, c = item
        return ds_kept.at[c, b * 4 + sub] if kind == BORROWED else ds_s.at[slot]

    def softmax_of(item, slot):
        b, sub, kind, c = item
        low = lowest(kind, sub)
        base = BLOCK if kind == FIRST else 0
        if low > base:
            ds_s[slot, base:low] = jnp.zeros((low - base, GROUP * SUB), jnp.bfloat16)
        ds_ref = ds_of(item, slot)
        for i in range(2):
            lanes = slice(i * HEAD, (i + 1) * HEAD)
            probs = softmax(item, slot, lanes)
            p_s[slot, low:, lanes] = probs.astype(jnp.bfloat16)
            ds_ref[low:, lanes] = dscores_of(probs, dp_buf[slot, low:, lanes])

    def query_gradient(item, ds_ref):
        b, sub, kind, c = item
        if kind == FIRST:
            keys = jnp.concatenate([kt_s[c, sub, b + 1], kt_s[c, sub, b + 2, :, :SUB]], axis=1)
            dq_t = jnp.dot(keys, ds_ref[BLOCK:], preferred_element_type=jnp.float32)
        else:
            keys = jnp.concatenate([kt_s[c, sub, b], kt_s[c, sub, b + 1]], axis=1)
            dq_t = jnp.dot(keys, ds_ref[: 2 * BLOCK], preferred_element_type=jnp.float32)
            dq_t = dq_t + jnp.dot(
                kt_s[c, sub, b + 2, :, :SUB], ds_ref[2 * BLOCK :], preferred_element_type=jnp.float32)
        dq = (dq_t * (scale * live_scale(b))).astype(jnp.bfloat16).T
        rows = rows_of(b, sub)
        for h in range(GROUP):
            at = pl.multiple_of(c * (GROUP * HEAD) + h * HEAD, HEAD)
            dq_ref[rows, pl.ds(at, HEAD)] = dq[h * SUB : (h + 1) * SUB]

    def key_sums(item, ds_ref):
        b, sub, kind, c = item
        low = lowest(kind, sub)
        dk_acc[c, window_of(b, sub, low), :] += jnp.dot(
            ds_ref[low:], stacked(q_s, b, sub, c), preferred_element_type=jnp.float32)

    def value_sums(item, half):
        b, sub, kind, c = item
        low = lowest(kind, sub)
        dv_acc[c, window_of(b, sub, low), :] += jnp.dot(
            half[low:], stacked(o_s, b, sub, c), preferred_element_type=jnp.float32)

    def gradients(item, slot):
        ds_ref = ds_of(item, slot)
        if item[2] != BORROWED:
            query_gradient(item, ds_ref)
        key_sums(item, ds_ref)
        value_sums(item, p_s.at[slot])

    def items_of(b, kind, c):
        return [(b, sub, kind, c) for sub in range(4)]

    def pipeline(items, old=(None, None), drain=False):
        chain = [*old, *items]
        for k, item in enumerate(items):
            scores_of(item, k % 2)
            if chain[k] is not None:
                gradients(chain[k], k % 2)
            if chain[k + 1] is not None:
                softmax_of(chain[k + 1], (k + 1) % 2)
        if drain:
            drain_of(items)

    def drain_of(items):
        gradients(items[-2], 0)
        softmax_of(items[-1], 1)
        gradients(items[-1], 1)

    def keys_transposed(c, first, last):
        for sub in range(4):
            for w in range(first, last):
                at = w * BLOCK + sub * SUB
                if at + BLOCK <= 640:
                    kt_s[c, sub, w] = k_s[c, pl.ds(at, BLOCK), :].T
                else:
                    kt_s[c, sub, w] = jnp.concatenate(
                        [k_s[c, pl.ds(at, 640 - at), :].T, jnp.zeros((HEAD, BLOCK - 640 + at), jnp.bfloat16)], axis=1)

    def remote_arrived(c, which):
        for part in range(2):
            @pl.when(receives[part])
            def _():
                for i in which:
                    remote(c, part)[i].wait_recv()

        if 0 in which:
            keys_transposed(c, 0, 2)

    def phase_one(blocks, c, then=None):
        items = [item for b in blocks for item in items_of(b, BORROWED, c)]
        for k in range(len(items) + 2):
            if k < len(items):
                s_buf[k % 2] = products(k_s, q_s, items[k])
            if k >= 2:
                value_sums(items[k - 2], p_half.at[k - 2])
            if 1 <= k < len(items) + 1:
                for i in range(2):
                    lanes = slice(i * HEAD, (i + 1) * HEAD)
                    probs = softmax(items[k - 1], (k - 1) % 2, lanes)
                    p_full[k - 1, :, lanes] = probs
                    p_half[k - 1, :, lanes] = probs.astype(jnp.bfloat16)
            if then is not None and k in then:
                then[k]()

    def phase_two(blocks, c, then=None):
        items = [item for b in blocks for item in items_of(b, BORROWED, c)]
        for k in range(len(items) + 2):
            if k < len(items):
                dp_buf[k % 2] = products(v_s, o_s, items[k])
            if k >= 2:
                key_sums(items[k - 2], ds_of(items[k - 2], k % 2))
            if 1 <= k < len(items) + 1:
                for i in range(2):
                    lanes = slice(i * HEAD, (i + 1) * HEAD)
                    ds_of(items[k - 1], (k - 1) % 2)[:, lanes] = dscores_of(
                        p_full[k - 1, :, lanes], dp_buf[(k - 1) % 2, :, lanes])
            if then is not None and k in then:
                then[k]()

    def kept_gradients(blocks, c):
        for b in blocks:
            for item in items_of(b, BORROWED, c):
                query_gradient(item, ds_of(item, 0))

    def wait_for(c, part, which=(0, 1)):
        for copy in remote(c, part, which):
            copy.wait_recv()

    def loop(first, last):
        def run(body):
            def step(c, carry):
                body(c)
                return carry

            lax.fori_loop(first, last, step, 0)

        return run

    last = KEYS - 1

    @pl.when(t == 0)
    def _():
        @loop(0, KEYS)
        def _(c):
            arrived(c)
            keys_transposed(c, 1, 2)
            pipeline(items_of(0, FIRST, c) + items_of(1, SECOND, c) + items_of(2, LATER, c), drain=True)

    @pl.when(t == 1)
    def _():
        def own(c):
            arrived(c)
            pipeline(items_of(1, FIRST, c) + items_of(2, SECOND, c), drain=True)

        loop(0, 2)(own)

        @loop(0, KEYS)
        def _(c):
            wait_for(c, 1, (0,))
            wait_for(c, 0, (0,))
            keys_transposed(c, 0, 2)
            phase_one((0,), c)
            send_back(c, 0, (1,))
            send_back(c, 1, (1,))
            wait_for(c, 1, (1,))
            wait_for(c, 0, (1,))
            phase_two((0,), c)
            send_back(c, 0, (0,))
            send_back(c, 1, (0,))

            @pl.when(c < 2)
            def _():
                own(c + 2)

        @loop(0, KEYS)
        def _(c):
            kept_gradients((0,), c)

    @pl.when(t == 2)
    def _():
        @loop(0, KEYS)
        def _(c):
            arrived(c)
            pipeline(items_of(2, FIRST, c), drain=True)

        @loop(0, KEYS)
        def _(c):
            wait_for(c, 1, (0,))
            wait_for(c, 0, (0,))
            keys_transposed(c, 0, 2)
            phase_one((0, 1), c, {5: lambda: send_back(c, 0, (1,))})
            send_back(c, 1, (1,))
            wait_for(c, 1, (1,))
            wait_for(c, 0, (1,))
            phase_two((0, 1), c, {5: lambda: send_back(c, 0, (0,)), 7: lambda: send_piece(c, 1, (0,))})
            send_piece(c, 2, (0,))

        @loop(0, KEYS)
        def _(c):
            kept_gradients((0, 1), c)

    @pl.when(t == 3)
    def _():
        def own(c, old=(None, None), drain=False):
            pipeline(items_of(2, LATER, c), old, drain)

        def shared(c, old):
            wait_for(c, 1)
            keys_transposed(c, 0, 2)
            pipeline(items_of(0, SECOND, c) + items_of(1, LATER, c), old)

        arrived(0)
        own(0)

        @loop(1, last)
        def _(c):
            arrived(c)
            own(c, items_of(2, LATER, c - 1)[2:])

        arrived(last)
        shared(0, items_of(2, LATER, last - 1)[2:])

        @loop(1, KEYS)
        def _(c):
            shared(c, items_of(1, LATER, c - 1)[2:])
            send_back(c - 1, 1, (0, 1))

        drain_of(items_of(1, LATER, last))
        send_back(last, 1, (0, 1))
        own(last, drain=True)

    def result(c, b):
        rows = pl.ds((b + 2) * BLOCK, BLOCK)
        dk = dk_acc[c, rows, :] * scale
        dv = dv_acc[c, rows, :]
        if b:
            dk = dk + k_in[c, pl.ds((b - 1) * BLOCK, BLOCK), :].astype(jnp.float32)
            dv = dv + v_in[c, pl.ds((b - 1) * BLOCK, BLOCK), :].astype(jnp.float32)
        alive = live_scale(b)
        dk_ref[b * BLOCK : (b + 1) * BLOCK, c * HEAD : (c + 1) * HEAD] = (dk * alive).astype(jnp.bfloat16)
        dv_ref[b * BLOCK : (b + 1) * BLOCK, c * HEAD : (c + 1) * HEAD] = (dv * alive).astype(jnp.bfloat16)

    for c in range(KEYS):
        result(c, 0)
    for c in range(KEYS):
        for part in range(2):
            @pl.when(sends[part])
            def _():
                for piece in pieces_of[part]:
                    for copy in back(c, piece):
                        copy.wait_recv()

            result(c, part + 1)

    for c in range(KEYS):
        for part in range(2):
            @pl.when(receives[part])
            def _():
                for piece in pieces_of[part]:
                    for copy in back(c, piece):
                        copy.wait_send()

            @pl.when(sends[part])
            def _():
                for copy in remote(c, part):
                    copy.wait_send()


def write_out(q_in, k_in, v_in, q_out, k_out, v_out, sem):
    copies = []
    for i in range(4):
        rows = pl.ds(96 * i, 96)
        copies.append(pltpu.make_async_copy(q_in.at[rows], q_out.at[rows], sem.at[i]))
    copies.append(pltpu.make_async_copy(k_in, k_out, sem.at[4]))
    copies.append(pltpu.make_async_copy(v_in, v_out, sem.at[5]))
    for copy in copies:
        copy.start()
    for copy in copies:
        copy.wait()


def local(queries, key_matrix, value_matrix, out_grads, seg_ids, bucket_dest):
    half, full = jnp.bfloat16, jnp.float32
    rows, q_width = queries.shape
    kv_width = key_matrix.shape[1]
    parts = pl.pallas_call(
        kernel,
        out_shape=(
            pltpu.VMEM((rows, q_width), half),
            pltpu.VMEM((rows, kv_width), half),
            pltpu.VMEM((rows, kv_width), half),
        ),
        in_specs=[pl.BlockSpec(memory_space=pltpu.HBM)] * 6,
        out_specs=[pl.BlockSpec(memory_space=pltpu.VMEM)] * 3,
        scratch_shapes=[
            pltpu.VMEM((KEYS, rows, GROUP * HEAD), half),
            pltpu.VMEM((KEYS, rows, GROUP * HEAD), half),
            pltpu.VMEM((KEYS, rows + 256, HEAD), half),
            pltpu.VMEM((KEYS, rows + 256, HEAD), half),
            pltpu.VMEM((KEYS, 4, 5, HEAD, BLOCK), half),
            pltpu.VMEM((12, WINDOW, 4 * SUB), full),
            pltpu.VMEM((2, WINDOW, GROUP * SUB), full),
            pltpu.VMEM((2, WINDOW, GROUP * SUB), full),
            pltpu.VMEM((2, WINDOW, GROUP * SUB), half),
            pltpu.VMEM((2, WINDOW, GROUP * SUB), half),
            pltpu.VMEM((8, WINDOW, GROUP * SUB), full),
            pltpu.VMEM((8, WINDOW, GROUP * SUB), half),
            pltpu.VMEM((KEYS, 8, WINDOW, GROUP * SUB), half),
            pltpu.VMEM((KEYS, rows + 256, HEAD), full),
            pltpu.VMEM((KEYS, rows + 256, HEAD), full),
            pltpu.VMEM((KEYS, 256, HEAD), half),
            pltpu.VMEM((KEYS, 256, HEAD), half),
            pltpu.VMEM((KEYS, 256, HEAD), half),
            pltpu.VMEM((KEYS, 256, HEAD), half),
            pltpu.VMEM((3, 512), jnp.int32),
            pltpu.SMEM((1, 3), jnp.int32),
            pltpu.SemaphoreType.DMA((KEYS, 4)),
            pltpu.SemaphoreType.DMA((2,)),
            pltpu.SemaphoreType.DMA((KEYS, 2, 2)),
            pltpu.SemaphoreType.DMA((KEYS, 2, 2)),
            pltpu.SemaphoreType.DMA((KEYS, 3, 2)),
            pltpu.SemaphoreType.DMA((KEYS, 3, 2)),
        ],
        compiler_params=pltpu.CompilerParams(
            collective_id=0, has_side_effects=True, vmem_limit_bytes=32 * 1024 * 1024
        ),
        name="packed_attention_backward",
    )(
        *[
            pltpu.with_memory_space_constraint(x, pltpu.HBM)
            for x in (queries, key_matrix, value_matrix, out_grads, seg_ids, bucket_dest)
        ]
    )
    return pl.pallas_call(
        write_out,
        out_shape=(
            jax.ShapeDtypeStruct((rows, q_width), half),
            jax.ShapeDtypeStruct((rows, kv_width), half),
            jax.ShapeDtypeStruct((rows, kv_width), half),
        ),
        in_specs=[pl.BlockSpec(memory_space=pltpu.VMEM)] * 3,
        out_specs=[pl.BlockSpec(memory_space=pltpu.HBM)] * 3,
        scratch_shapes=[pltpu.SemaphoreType.DMA((6,))],
        compiler_params=pltpu.CompilerParams(vmem_limit_bytes=4 * 1024 * 1024),
        name="write_out",
    )(*[pltpu.with_memory_space_constraint(p, pltpu.VMEM) for p in parts])


def solution(mesh):
    in_specs = (
        P(("dp", "tensor"), None),
        P(("dp", "tensor"), None),
        P(("dp", "tensor"), None),
        P(("dp", "tensor"), None),
        P("dp", None),
        P("dp", None),
    )
    out_specs = (P(("dp", "tensor"), None), P(("dp", "tensor"), None), P(("dp", "tensor"), None))
    return jax.shard_map(local, mesh=mesh, in_specs=in_specs, out_specs=out_specs, check_vma=False)
```
